32 devices in a mesh: hst: 8 (over z, x), tp: 4 (over y, core).
Axes of the slice: x: 2, y: 2, z: 4, core: 2. Of those that a mesh axis runs over, the one named last changes fastest.
Arguments:
- queries: bfloat16 [512, 4096], P('hst', 'tp')
- key_page_cache: bfloat16 [4096, 16, 1024], P('hst', None, 'tp')
- value_page_cache: bfloat16 [4096, 16, 1024], P('hst', None, 'tp'), may hold values from -5 to 5
- request_pages: int32 [512, 8], P('hst'), may hold values from 0 to 511, as said below
- context_length: int32 [512], P('hst'), may hold values from 2 to 128, as said below
- output_weight: bfloat16 [4096, 4096], P('tp'), may hold values from -0.09375 to 0.09375
- adapter_down_weight: bfloat16 [256, 64, 4096], P('hst', None, 'tp'), may hold values from -0.09375 to 0.09375
- adapter_up_weight: bfloat16 [256, 64, 4096], P('hst', None, 'tp'), may hold values from -0.75 to 0.75
- residual: bfloat16 [512, 4096], P('hst', 'tp'), may hold values from -6 to 6
- host_slot_adapter: int32 [256], P('hst'), may hold values from 0 to 255, as said below
- request_slot: int32 [512, 1], P('hst'), may hold values from 0 to 31; in each aligned block of 64 rows (0 to 63, 64 to 127, ...) at most 4 rows name the same one
Outputs:
- hidden_out: bfloat16 [512, 4096], P('hst', 'tp')
The draws below stay inside these ranges and needn't reach their ends.
Inputs may be any that keep to these rules, and one draw needn't show every extreme that they name: `request_pages`: entries of one host are its pages 512 in some order: every page of the host belongs to exactly one request. `context_length`: some request of every host has exactly 128 cached tokens. `host_slot_adapter`: A host's 32 entries name different adapters; adapter a is owned by host a // 32. No owner serves more than 8 slots of one host, and some owner serves exactly 8 slots of every host. `request_slot`: at most 4 of the rows of one host name one slot.
All inputs are finite; a program needn't handle non-finite values.
Results may differ from the reference program's by a relative error of at most 0.0085.
Values may be sent and summed in bfloat16 or wider, within the bound.
No kernel may reach another device: no remote copies, remote signals or barrier semaphores. Data moves between devices by JAX's collectives and lax.ppermute only.
A program may use at most 128 MiB of HBM per device.

```python
import math
import jax
import jax.numpy as jnp
import numpy as np
from jax import lax

MODEL_WIDTH = 4096
H = 32
KVH = 8
HD = 128
ADAPTER_RANK = 64
PAGE = 16
SLOTS = 32
ROWS = 64
CTX = 128
ADP_HOST = 32
ADAPTER_TOTAL = 256
ROWS_ALL = 512
MAXP = 8
PAGES = 512
MOST = 8
CAP = 4
N_HST = 8


def page_order(key):
    subkey = jax.random.fold_in(key, 7)
    host_count = ADAPTER_TOTAL // ADP_HOST
    host_keys = jax.random.split(subkey, host_count)
    orders = jax.vmap(lambda one_key: jax.random.permutation(one_key, PAGES))(host_keys)
    return orders.reshape(host_count * ROWS, MAXP).astype(jnp.int32)


def draw_request_pages(key, part):
    return page_order(key)


def draw_key_page_cache(key, part):
    key = jax.random.fold_in(key, 23)
    host_count = ADAPTER_TOTAL // ADP_HOST
    keys_all = jnp.clip(jax.random.normal(key, (host_count * PAGES, PAGE, KVH * HD), jnp.float32), -4.0, 4.0)
    return keys_all.astype(jnp.bfloat16)


def draw_queries(key, part):
    key = jax.random.fold_in(key, 29)
    host_count = ADAPTER_TOTAL // ADP_HOST
    row_total = host_count * ROWS
    query_all = jnp.clip(jax.random.normal(key, (row_total, H * HD), jnp.float32), -4.0, 4.0)
    return query_all.astype(jnp.bfloat16)


def draw_context_length(key, part):
    key = jax.random.fold_in(key, 31)
    host_count = ADAPTER_TOTAL // ADP_HOST
    lengths = jax.random.randint(key, (host_count, ROWS), 2, CTX + 1)
    full_row = jax.random.randint(jax.random.fold_in(key, 1), (host_count,), 0, ROWS)
    lengths = jnp.where(jnp.arange(ROWS)[None, :] == full_row[:, None], CTX, lengths)
    return lengths.reshape(host_count * ROWS).astype(jnp.int32)


def draw_host_slot_adapter(key, part):
    key = jax.random.fold_in(key, 37)
    host_count = ADAPTER_TOTAL // ADP_HOST
    lowrank_stock_count = host_count * MOST
    lowrank_holder_device = jnp.arange(lowrank_stock_count) // MOST
    pool_copy = jnp.arange(lowrank_stock_count) % MOST
    preferred_machine = jax.random.randint(jax.random.fold_in(key, 1), (), 0, host_count)
    machine_leaning = jax.random.randint(jax.random.fold_in(key, 2), (host_count,), 0, 4)
    noise_perturbation = jax.random.randint(jax.random.fold_in(key, 3), (host_count, lowrank_stock_count), 0, 2 ** 15)
    liking_boost = machine_leaning[lowrank_holder_device] * 2 ** 14 + (lowrank_holder_device == preferred_machine).astype(jnp.int32) * 2 ** 20
    query_match_logits = (noise_perturbation + liking_boost[None, :]) * lowrank_stock_count + jnp.arange(lowrank_stock_count)[None, :]
    top_scores, picked_adapters = lax.top_k(query_match_logits, SLOTS)
    owners = lowrank_holder_device[picked_adapters]
    copies = pool_copy[picked_adapters]
    shifts = jax.random.randint(jax.random.fold_in(key, 4), (host_count, host_count), 0, ADP_HOST)
    offsets = jnp.take_along_axis(shifts, owners, axis=1)
    adapter_ids = owners * ADP_HOST + (copies + offsets) % ADP_HOST
    host_keys = jax.random.split(jax.random.fold_in(key, 5), host_count)
    shuffled = jax.vmap(lambda one_key, id_row: jax.random.permutation(one_key, id_row))(host_keys, adapter_ids)
    return shuffled.reshape(host_count * SLOTS).astype(jnp.int32)


def block_levels(own_key, dims, pieces, low, top_value):
    def one(dim, blocks):
        heights = jax.random.uniform(jax.random.fold_in(jax.random.fold_in(own_key, 6), dim), (blocks,), jnp.float32, low / len(pieces), top_value / len(pieces))
        return jnp.repeat(jnp.exp(heights), dims[dim] // blocks).reshape((-1,) + (1,) * (len(dims) - dim - 1))

    factor_of = one(*pieces[0])
    for cut in pieces[1:]:
        factor_of = factor_of * one(*cut)
    return factor_of


def assign_block(key, own, number, rows, number_of, top, limit, lean):
    sequence = jax.random.permutation(key, number_of)
    packed, usual = shares(number_of, rows * top, limit, lean, True), shares(number_of, rows * top, limit, lean, False)
    places = jnp.arange(number_of)

    def named(sizes, turn):
        used = int((sizes > 0).sum())
        fixed = max(1, used // 4)
        shifted = fixed + (places - fixed + turn * (used - fixed)) % max(1, number_of - fixed)
        return jnp.zeros((number_of,), jnp.int32).at[sequence[jnp.where(places < fixed, places, shifted)]].set(jnp.asarray(sizes, jnp.int32))

    sizes = jnp.where(number % 4 == 0, named(packed, number // 4), named(usual, number - number // 4 - 1))
    mixed = jax.random.permutation(jax.random.fold_in(own, 3), number_of)
    source_of, taker = mixed[0:number_of // 2 * 2:2], mixed[1:number_of // 2 * 2:2]
    slack = jnp.minimum(sizes[source_of] - 1, limit - sizes[taker]) // 2
    slack = jnp.where((source_of == sequence[0]) | (taker == sequence[0]) | (sizes[taker] == 0), 0, jnp.maximum(slack, 0))
    shifted = jax.random.randint(jax.random.fold_in(own, 4), (number_of // 2,), 0, 1 << 20) % (slack + 1)
    sizes = sizes.at[source_of].add(-shifted).at[taker].add(shifted)
    members = jnp.searchsorted(jnp.cumsum(sizes), jnp.arange(rows * top), side="right").astype(jnp.int32)
    listing = members.reshape(top, rows).T
    listing = listing[jax.random.permutation(jax.random.fold_in(own, 1), rows)]
    turn = jax.random.randint(jax.random.fold_in(own, 2), (rows, 1), 0, top)
    return jnp.take_along_axis(listing, (jnp.arange(top)[None, :] + turn) % top, axis=1)


def shares(amount, total, bound, skew, full):
    portions = [(1 << 20) // math.isqrt(grade ** skew) + 1 for grade in range(1, amount + 1)]
    largest = bound if full else min(bound, max(-(-total // amount), total * portions[0] // sum(portions)))
    least = 1 if total - largest >= amount - 1 else 0
    holding, surplus = [largest] + [least] * (amount - 1), total - largest - least * (amount - 1)
    while surplus > 0:
        movable = [i for i in range(1, amount) if holding[i] < largest] or [i for i in range(1, amount) if holding[i] < bound]
        mass, budget = sum([portions[i] for i in movable]), surplus
        for i in movable:
            more = min(bound - holding[i], max(1, budget * portions[i] // mass), surplus)
            holding[i] = holding[i] + more
            surplus = surplus - more
    return np.array(holding)


def noise(rng, extent, width, bound, pieces=(), held_as=jnp.bfloat16):
    result = jax.random.normal(rng, extent, jnp.float32) * width
    if len(pieces) > 0:
        result = block_levels(rng, extent, pieces, -0.22, 0.18) * result
    return jnp.clip(result, min=-bound, max=bound).astype(held_as)


def setup_inputs(seed: int = 0) -> dict:
    splits = jax.random.split(jax.random.key(seed), 12)
    queries = draw_queries(jax.random.fold_in(splits[11], 71), 0)
    key_page_cache = draw_key_page_cache(jax.random.fold_in(splits[11], 71), 0)
    value_page_cache = noise(splits[2], (N_HST * PAGES, PAGE, KVH * HD), 1.0, 5.0, ((0, 8), (2, 4)))
    request_pages = draw_request_pages(jax.random.fold_in(splits[11], 71), 0)
    context_length = draw_context_length(jax.random.fold_in(splits[11], 71), 0)
    output_weight = noise(splits[5], (MODEL_WIDTH, MODEL_WIDTH), MODEL_WIDTH ** -0.5, 0.09375, ((0, 4),))
    adapter_down_weight = noise(splits[6], (ADAPTER_TOTAL, ADAPTER_RANK, MODEL_WIDTH), MODEL_WIDTH ** -0.5, 0.09375, ((0, 8), (2, 4)))
    adapter_up_weight = noise(splits[7], (ADAPTER_TOTAL, ADAPTER_RANK, MODEL_WIDTH), ADAPTER_RANK ** -0.5, 0.75, ((0, 8), (2, 4)))
    residual = noise(splits[8], (ROWS_ALL, MODEL_WIDTH), 1.0, 6.0, ((0, 8), (1, 4)))
    host_slot_adapter = draw_host_slot_adapter(jax.random.fold_in(splits[11], 71), 0)
    request_slot_keys = jax.random.split(jax.random.fold_in(splits[10], 1), ROWS_ALL // ROWS)
    request_slot_turns = jax.random.permutation(jax.random.fold_in(splits[10], 3), ROWS_ALL // ROWS)
    request_slot = jax.vmap(lambda own, number: assign_block(jax.random.fold_in(splits[10], 2), own, number, ROWS, SLOTS, 1, CAP, 1))(request_slot_keys, request_slot_turns).reshape((ROWS_ALL, 1))
    return {"queries": queries, "key_page_cache": key_page_cache, "value_page_cache": value_page_cache, "request_pages": request_pages, "context_length": context_length, "output_weight": output_weight, "adapter_down_weight": adapter_down_weight, "adapter_up_weight": adapter_up_weight, "residual": residual, "host_slot_adapter": host_slot_adapter, "request_slot": request_slot}


ADAPTER_SCALE = 2.0

def reference(queries, key_page_cache, value_page_cache, request_pages, context_length, output_weight, adapter_down_weight, adapter_up_weight, residual, host_slot_adapter, request_slot):
    group_size = H // KVH

    def one_host(host_index):
        row_start = host_index * ROWS
        query_rows = lax.dynamic_slice_in_dim(queries, row_start, ROWS, 0).astype(jnp.float32).reshape(ROWS, KVH, group_size, HD)
        page_rows = lax.dynamic_slice_in_dim(request_pages, row_start, ROWS, 0) + host_index * PAGES
        key_rows = key_page_cache[page_rows].astype(jnp.float32).reshape(ROWS, CTX, KVH, HD)
        value_rows = value_page_cache[page_rows].astype(jnp.float32).reshape(ROWS, CTX, KVH, HD)
        lengths = lax.dynamic_slice_in_dim(context_length, row_start, ROWS, 0)
        query_match_logits = jnp.einsum('rkgd,rtkd->rkgt', query_rows, key_rows) / math.sqrt(HD)
        live_mask = jnp.arange(CTX)[None, :] < lengths[:, None]
        query_match_logits = jnp.where(live_mask[:, None, None, :], query_match_logits, -jnp.inf)
        attn_weights = jax.nn.softmax(query_match_logits, axis=-1).astype(jnp.bfloat16)
        attended = jnp.einsum('rkgt,rtkd->rkgd', attn_weights.astype(jnp.float32), value_rows)
        attended = attended.astype(jnp.bfloat16).reshape(ROWS, MODEL_WIDTH)
        slot_ids = lax.dynamic_slice_in_dim(host_slot_adapter, host_index * SLOTS, SLOTS, 0)
        chosen = lax.dynamic_slice_in_dim(request_slot, row_start, ROWS, 0)[:, 0]
        adapter_index = slot_ids[chosen]
        down_weight_rows = adapter_down_weight[adapter_index].astype(jnp.float32)
        reduced_activations = jnp.einsum('rd,rkd->rk', attended.astype(jnp.float32), down_weight_rows).astype(jnp.bfloat16)
        up_weight_rows = adapter_up_weight[adapter_index].astype(jnp.float32)
        adapter_rows = jnp.einsum('lw,lwn->ln', reduced_activations.astype(jnp.float32), up_weight_rows)
        base_output = jnp.dot(attended, output_weight, preferred_element_type=jnp.float32)
        residual_output_rows = lax.dynamic_slice_in_dim(residual, row_start, ROWS, 0).astype(jnp.float32)
        return (residual_output_rows + base_output + ADAPTER_SCALE * adapter_rows).astype(jnp.bfloat16)
    stacked = lax.map(one_host, jnp.arange(N_HST).astype(jnp.int32))
    return stacked.reshape(N_HST * ROWS, MODEL_WIDTH)
```

```python
import functools
import math

import jax
import jax.numpy as jnp
from jax import lax
from jax.experimental import pallas as pl
from jax.experimental.pallas import tpu as pltpu
from jax.sharding import PartitionSpec as P

HD = 128
LANES = 128
HEAD_ROWS = 8
GROUP = 16
ADAPTER_SCALE = 2.0
CAP = 4
FIRST = 20
CHUNKS = 4

MIB = 1 << 20
NT = (((1,), (1,)), ((), ()))
TN = (((0,), (0,)), ((), ()))
NN = (((1,), (0,)), ((), ()))


def iota(shape, axis):
    return lax.broadcasted_iota(jnp.int32, shape, axis)


def pair_rows(slot_total, host_count):
    return CAP * (2 * slot_total // host_count)


def up_to(value, step):
    return -(-value // step) * step


def copies(source, target, sem, count):
    cut = source.shape[0] // count
    return [
        pltpu.make_async_copy(
            source.at[pl.ds(i * cut, cut)], target.at[pl.ds(i * cut, cut)], sem.at[i]
        )
        for i in range(count)
    ]


def in_hbm(*arrays):
    return [pltpu.with_memory_space_constraint(a, pltpu.HBM) for a in arrays]


def attention_kernel(owned_total, host_count, tp_count, room, *refs):
    pages_hbm, length_hbm, query_hbm, slot_hbm, stock_hbm, keys_hbm, values_hbm = refs[:7]
    down_hbm, output_hbm, attended_ref, place_ref, down_ref = refs[7:12]
    evens = tp_count // 2
    even_refs, odd_ref, refs = refs[12 : 12 + evens], refs[12 + evens], refs[13 + evens :]
    block_refs, refs = refs[:host_count], refs[host_count:]
    (
        pages_ref,
        length_ref,
        query_ref,
        slot_ref,
        stock_ref,
        keys,
        values,
        output,
        query_rows,
        outcome,
        packed,
        numbers,
        counts,
        small_sem,
        key_sem,
        value_sem,
        down_sem,
        output_sem,
    ) = refs
    row_count, feature_here = query_ref.shape
    page_total, page, kv_width = keys_hbm.shape
    heads = feature_here // HD
    kv_here = kv_width // HD
    share = heads // kv_here
    most_pages = pages_ref.shape[0]
    context = most_pages * page

    small_moves = [
        pltpu.make_async_copy(source, target, small_sem.at[i])
        for i, (source, target) in enumerate(
            (
                (query_hbm, query_ref),
                (slot_hbm, slot_ref),
                (stock_hbm, stock_ref),
                (pages_hbm, pages_ref),
                (length_hbm, length_ref),
            )
        )
    ]
    key_moves = copies(keys_hbm, keys, key_sem, CHUNKS)
    value_moves = copies(values_hbm, values, value_sem, CHUNKS)
    down_moves = copies(down_hbm, down_ref, down_sem, CHUNKS)
    width = output_hbm.shape[1] // tp_count
    output_moves = []
    for k in range(tp_count):
        columns = pl.ds(pl.multiple_of((lax.axis_index("tp") ^ k) * width, width), width)
        output_moves.append(copies(output_hbm.at[:, columns], output.at[k], output_sem.at[k], 2))
    for move in small_moves + key_moves:
        move.start()
    packed[...] = jnp.zeros_like(packed)
    numbers[...] = jnp.zeros_like(numbers)
    for o in range(host_count):
        counts[o] = 0
    for move in small_moves:
        move.wait()

    if heads < HEAD_ROWS:
        query_rows[...] = jnp.zeros_like(query_rows)
    for j in range(heads):
        query_rows[pl.ds(j, row_count, stride=HEAD_ROWS), :] = query_ref[
            :, j * HD : (j + 1) * HD
        ].astype(jnp.float32)

    me = lax.axis_index("hst")
    pad = up_to(room, 8)

    def count(r, most):
        adapter = stock_ref[0, slot_ref[0, r]]
        owner = lax.div(adapter, owned_total)
        before = counts[owner]
        counts[owner] = before + 1
        block = owner ^ me
        fits = before < room
        place_ref[r] = jnp.where(fits, block * room + before, host_count * room)
        where = jnp.where(fits, block * pad + before, host_count * pad)
        number = jnp.full((1, LANES), adapter - owner * owned_total + 1, jnp.int32)
        numbers[pl.ds(where, 1), :] = number.astype(jnp.float32)
        return jnp.maximum(most, before)

    most = lax.fori_loop(0, row_count, count, jnp.int32(0))
    over = jnp.where(jnp.full((8, LANES), most, jnp.int32) >= room, 1.0, 0.0)

    for move in key_moves[: CHUNKS // 2]:
        move.wait()
    for move in value_moves:
        move.start()
    for move in key_moves[CHUNKS // 2 :]:
        move.wait()

    head_of = iota((HEAD_ROWS, HD), 0) // share

    def tile_of(r):
        return pl.ds(pl.multiple_of(r * HEAD_ROWS, HEAD_ROWS), HEAD_ROWS)

    def some_scores(step, carry):
        first = step * GROUP
        scores = []
        for i in range(GROUP):
            r = first + i
            rows = query_rows[tile_of(r), :]
            wide = jnp.concatenate(
                [jnp.where(head_of == c, rows, 0.0) for c in range(kv_here)], axis=1
            ).astype(jnp.bfloat16)
            held = jnp.concatenate([keys[pages_ref[p, r]] for p in range(most_pages)], axis=0)
            part = lax.dot_general(wide, held, NT, preferred_element_type=jnp.float32)
            live = iota((HEAD_ROWS, context), 1) < length_ref[r]
            scores.append(jnp.where(live, part * (1.0 / math.sqrt(HD)), -jnp.inf))
        score = jnp.concatenate(scores, axis=0)
        weight = jnp.exp(score - jnp.max(score, axis=1, keepdims=True))
        weight = weight / jnp.sum(weight, axis=1, keepdims=True)
        size = GROUP * HEAD_ROWS
        outcome[pl.ds(pl.multiple_of(step * size, size), size), :] = weight
        return carry

    def some_values(step, carry):
        first = step * GROUP
        for i in range(GROUP):
            r = first + i
            held = jnp.concatenate([values[pages_ref[p, r]] for p in range(most_pages)], axis=0)
            part = lax.dot_general(
                outcome[tile_of(r), :].astype(jnp.bfloat16),
                held,
                NN,
                preferred_element_type=jnp.float32,
            )
            result = part[:, :HD]
            for c in range(1, kv_here):
                result = jnp.where(head_of == c, part[:, c * HD : (c + 1) * HD], result)
            outcome[tile_of(r), :] = result
            packed[tile_of(place_ref[r]), :] = result
        return carry

    lax.fori_loop(0, row_count // GROUP, some_scores, 0)
    for move in value_moves[: CHUNKS // 2]:
        move.wait()
    for moves in output_moves:
        for move in moves:
            move.start()
    for move in value_moves[CHUNKS // 2 :]:
        move.wait()
    lax.fori_loop(0, row_count // GROUP, some_values, 0)
    for move in down_moves:
        move.start()

    lane = iota((8, LANES), 1)
    size = room * HEAD_ROWS
    for k in range(host_count):
        tile = jnp.where(lane == LANES - 1, over, 0.0)
        for b in range(pad // 8):
            tile = jnp.where(lane == b, numbers[k * pad + 8 * b : k * pad + 8 * b + 8], tile)
        block_refs[k][...] = jnp.concatenate(
            [packed[k * size : (k + 1) * size], tile], axis=0
        ).astype(jnp.bfloat16)
    for j in range(heads):
        attended_ref[:, j * HD : (j + 1) * HD] = outcome[
            pl.ds(j, row_count, stride=HEAD_ROWS), :
        ].astype(jnp.bfloat16)
    rows = attended_ref[...]
    for k in range(tp_count):
        for move in output_moves[k]:
            move.wait()
        product = jnp.dot(rows, output[k], preferred_element_type=jnp.float32)
        if k % 2 == 0:
            even_refs[k // 2][...] = product.astype(jnp.bfloat16)
        else:
            first = k // 2 * row_count
            odd_ref[first : first + row_count] = product.astype(jnp.bfloat16)
    for move in down_moves:
        move.wait()


def attend(
    queries, keys, values, pages, lengths, slots, stock, down, output, owned_total, hosts, room
):
    row_count, feature_here = queries.shape
    tp_count = output.shape[1] // feature_here
    spec = pl.BlockSpec(memory_space=pltpu.VMEM)
    small = pl.BlockSpec(memory_space=pltpu.SMEM)
    far = pl.BlockSpec(memory_space=pl.ANY)
    evens = tp_count // 2
    base = jax.ShapeDtypeStruct((row_count, feature_here), jnp.bfloat16)
    odd = jax.ShapeDtypeStruct((evens * row_count, feature_here), jnp.bfloat16)
    block = jax.ShapeDtypeStruct((room * HEAD_ROWS + 8, LANES), jnp.bfloat16)
    outs = pl.pallas_call(
        functools.partial(attention_kernel, owned_total, hosts, tp_count, room),
        name="attend",
        out_shape=[
            jax.ShapeDtypeStruct((row_count, feature_here), jnp.bfloat16),
            jax.ShapeDtypeStruct((row_count,), jnp.int32),
            pltpu.VMEM(down.shape, jnp.bfloat16),
        ]
        + [base] * evens
        + [odd]
        + [block] * hosts,
        in_specs=[far] * 9,
        out_specs=[spec, small, spec] + [spec] * (evens + 1 + hosts),
        scratch_shapes=[
            pltpu.SMEM(pages.shape, jnp.int32),
            pltpu.SMEM(lengths.shape, jnp.int32),
            pltpu.VMEM(queries.shape, jnp.bfloat16),
            pltpu.SMEM(slots.shape, jnp.int32),
            pltpu.SMEM(stock.shape, jnp.int32),
            pltpu.VMEM(keys.shape, jnp.bfloat16),
            pltpu.VMEM(values.shape, jnp.bfloat16),
            pltpu.VMEM((tp_count, feature_here, feature_here), jnp.bfloat16),
            pltpu.VMEM((row_count * HEAD_ROWS, HD), jnp.float32),
            pltpu.VMEM((row_count * HEAD_ROWS, HD), jnp.float32),
            pltpu.VMEM(((hosts * room + 1) * HEAD_ROWS, HD), jnp.float32),
            pltpu.VMEM((hosts * up_to(room, 8) + 8, LANES), jnp.float32),
            pltpu.SMEM((hosts,), jnp.int32),
            pltpu.SemaphoreType.DMA((5,)),
            pltpu.SemaphoreType.DMA((CHUNKS,)),
            pltpu.SemaphoreType.DMA((CHUNKS,)),
            pltpu.SemaphoreType.DMA((CHUNKS,)),
            pltpu.SemaphoreType.DMA((tp_count, 2)),
        ],
        compiler_params=pltpu.CompilerParams(vmem_limit_bytes=32 * MIB),
        cost_estimate=pl.CostEstimate(
            flops=4 * row_count * HEAD_ROWS * 128 * feature_here,
            bytes_accessed=4 * keys.size + 2 * output.size + 2 * down.size,
            transcendentals=row_count * HEAD_ROWS * 128,
        ),
    )(*in_hbm(pages, lengths, queries, slots, stock, keys, values, down, output))
    return outs[:3], outs[3 : 3 + evens], outs[3 + evens], outs[4 + evens :]


def shrink_kernel(host_count, room, *refs):
    blocks = refs[:host_count]
    down_ref, up_hbm, partial_ref, number_ref, over_ref, up_ref = refs[host_count : host_count + 6]
    tiles, total, up_sem = refs[host_count + 6 :]
    up_moves = copies(up_hbm, up_ref, up_sem, CHUNKS)
    for move in up_moves:
        move.start()
    heads = down_ref.shape[1] // HD
    rows_all = host_count * room
    size = room * HEAD_ROWS
    width = 256
    rank = LANES // 2
    over = jnp.float32(0)
    lane = iota((8, LANES), 1)
    for k in range(host_count):
        tiles[k * size : (k + 1) * size] = blocks[k][:size].astype(jnp.float32)
        tile = blocks[k][size:].astype(jnp.float32)
        over = jnp.maximum(over, jnp.max(jnp.where(lane == LANES - 1, tile, 0.0)))
        for b in range(up_to(room, 8) // 8):
            rest = min(8, room - 8 * b)
            column = jnp.sum(jnp.where(lane == b, tile, 0.0), axis=1, keepdims=True)
            column = jnp.broadcast_to(column, (8, LANES))
            number_ref[k * room + 8 * b : k * room + 8 * b + rest] = column[:rest]
    over_ref[0] = (over > 0).astype(jnp.int32)
    rows = jnp.concatenate(
        [tiles[pl.ds(j, rows_all, stride=HEAD_ROWS), :].astype(jnp.bfloat16) for j in range(heads)],
        axis=1,
    )
    number = number_ref[...]
    own = (iota(number.shape, 1) // rank).astype(jnp.float32) + 1.0
    for step in range(down_ref.shape[0] // width):
        product = lax.dot_general(
            rows,
            down_ref[step * width : (step + 1) * width],
            NT,
            preferred_element_type=jnp.float32,
        )
        add = jnp.zeros_like(number) if step == 0 else total[...]
        for i in range(width // LANES):
            piece = product[:, i * LANES : (i + 1) * LANES]
            first = 2.0 * (step * (width // LANES) + i)
            add = jnp.where(number == own + first, piece + add, add)
        total[...] = add
    full = total[...]
    full = full + pltpu.roll(full, rank, 1)
    half = rows_all // 2
    left = iota((half, LANES), 1) < rank
    partial_ref[...] = jnp.where(left, full[:half], full[half:]).astype(jnp.bfloat16)
    for move in up_moves:
        move.wait()


def shrink(blocks, down, up, room):
    host_count = len(blocks)
    rows = host_count * room
    spec = pl.BlockSpec(memory_space=pltpu.VMEM)
    return pl.pallas_call(
        functools.partial(shrink_kernel, host_count, room),
        name="shrink",
        out_shape=(
            jax.ShapeDtypeStruct((rows // 2, LANES), jnp.bfloat16),
            jax.ShapeDtypeStruct((rows, LANES), jnp.float32),
            jax.ShapeDtypeStruct((1,), jnp.int32),
            pltpu.VMEM(up.shape, jnp.bfloat16),
        ),
        in_specs=[spec] * (host_count + 1) + [pl.BlockSpec(memory_space=pl.ANY)],
        out_specs=(spec, spec, pl.BlockSpec(memory_space=pltpu.SMEM), spec),
        scratch_shapes=[
            pltpu.VMEM((rows * HEAD_ROWS, HD), jnp.float32),
            pltpu.VMEM((rows, LANES), jnp.float32),
            pltpu.SemaphoreType.DMA((CHUNKS,)),
        ],
        compiler_params=pltpu.CompilerParams(vmem_limit_bytes=12 * MIB),
        cost_estimate=pl.CostEstimate(
            flops=2 * rows * down.size, bytes_accessed=2 * down.size, transcendentals=0
        ),
    )(*blocks, down, *in_hbm(up))


def expand_kernel(part_count, host_count, *refs):
    parts, (number_ref, up_ref) = refs[:part_count], refs[part_count : part_count + 2]
    outs, (spread, tiles) = refs[part_count + 2 : -2], refs[-2:]
    rows, columns = number_ref.shape[0], up_ref.shape[1]
    width = min(256, columns)
    rank = LANES // 2
    full = parts[0][...].astype(jnp.float32)
    for p in parts[1:]:
        full = full + p[...].astype(jnp.float32)
    other = pltpu.roll(full, rank, 1)
    left = iota(full.shape, 1) < rank
    both = jnp.concatenate(
        [jnp.where(left, full, other), jnp.where(left, other, full)], axis=0
    )
    number = number_ref[...]
    own = (iota(number.shape, 1) // rank).astype(jnp.float32) + 1.0
    for i in range(spread.shape[1] // LANES):
        spread[:, i * LANES : (i + 1) * LANES] = jnp.where(
            number == own + 2.0 * i, both, 0.0
        ).astype(jnp.bfloat16)
    if columns // HD < HEAD_ROWS:
        tiles[...] = jnp.zeros_like(tiles)
    for i in range(columns // width):
        result = jnp.dot(
            spread[...],
            up_ref[:, i * width : (i + 1) * width],
            preferred_element_type=jnp.float32,
        )
        for j in range(width // HD):
            tiles[pl.ds(i * (width // HD) + j, rows, stride=HEAD_ROWS), :] = result[
                :, j * HD : (j + 1) * HD
            ]
    size = rows // host_count * HEAD_ROWS
    for k in range(host_count):
        outs[k][...] = tiles[k * size : (k + 1) * size].astype(jnp.bfloat16)


def expand(parts, number, up, host_count):
    rows = number.shape[0]
    depth, columns = up.shape
    spec = pl.BlockSpec(memory_space=pltpu.VMEM)
    block = jax.ShapeDtypeStruct((rows // host_count * HEAD_ROWS, HD), jnp.bfloat16)
    return pl.pallas_call(
        functools.partial(expand_kernel, len(parts), host_count),
        name="expand",
        out_shape=[block] * host_count,
        in_specs=[spec] * (len(parts) + 2),
        out_specs=[spec] * host_count,
        scratch_shapes=[
            pltpu.VMEM((rows, depth), jnp.bfloat16),
            pltpu.VMEM((rows * HEAD_ROWS, HD), jnp.float32),
        ],
        compiler_params=pltpu.CompilerParams(vmem_limit_bytes=12 * MIB),
        cost_estimate=pl.CostEstimate(
            flops=2 * rows * up.size, bytes_accessed=2 * up.size, transcendentals=0
        ),
    )(*parts, number, up)


def finish_kernel(base_count, back_count, place_ref, residual_ref, *refs):
    bases, backs = refs[:base_count], refs[base_count : base_count + back_count]
    more, (out_ref, tiles, sorted_tiles) = refs[base_count + back_count : -3], refs[-3:]
    row_count, columns = residual_ref.shape
    size = backs[0].shape[0]
    for k in range(back_count):
        tiles[k * size : (k + 1) * size] = backs[k][...].astype(jnp.float32)
    tiles[back_count * size :] = jnp.zeros((HEAD_ROWS, HD), jnp.float32)
    for r in range(row_count):
        where = pl.multiple_of(place_ref[r] * HEAD_ROWS, HEAD_ROWS)
        sorted_tiles[r * HEAD_ROWS : (r + 1) * HEAD_ROWS] = tiles[pl.ds(where, HEAD_ROWS), :]
    for j in range(columns // HD):
        cut = slice(j * HD, (j + 1) * HD)
        total = sorted_tiles[pl.ds(j, row_count, stride=HEAD_ROWS), :]
        for m in more:
            total = total + m[:, cut]
        total = residual_ref[:, cut].astype(jnp.float32) + ADAPTER_SCALE * total
        for b in bases:
            total = total + b[:row_count, cut].astype(jnp.float32)
        out_ref[:, cut] = total.astype(jnp.bfloat16)


def finish(place, residual, bases, backs, *more):
    spec = pl.BlockSpec(memory_space=pltpu.VMEM)
    size = backs[0].shape[0]
    return pl.pallas_call(
        functools.partial(finish_kernel, len(bases), len(backs)),
        name="finish",
        out_shape=pltpu.HBM(residual.shape, jnp.bfloat16),
        in_specs=[pl.BlockSpec(memory_space=pltpu.SMEM)]
        + [spec] * (1 + len(bases) + len(backs) + len(more)),
        out_specs=spec,
        scratch_shapes=[
            pltpu.VMEM((len(backs) * size + HEAD_ROWS, HD), jnp.float32),
            pltpu.VMEM((residual.shape[0] * HEAD_ROWS, HD), jnp.float32),
        ],
        compiler_params=pltpu.CompilerParams(vmem_limit_bytes=8 * MIB),
    )(place, residual, *bases, *backs, *more)


def swap(value, axis, k):
    size = lax.axis_size(axis)
    return lax.ppermute(value, axis, [(i, i ^ k) for i in range(size)])


def swap_all(values, axis):
    return [values[0]] + [swap(values[k], axis, k) for k in range(1, len(values))]


def second_pass(attended, down, up, stock, slots, room, rest):
    owned_total, rank, feature_here = down.shape
    host_count = lax.axis_size("hst")
    tp_count = lax.axis_size("tp")
    row_count = attended.shape[0]
    adapter = stock[slots]
    owner = adapter // owned_total
    order = jnp.arange(row_count)
    same = (owner[:, None] == owner[None, :]) & (order[None, :] < order[:, None])
    before = jnp.sum(same, axis=1)
    target = jnp.where(before >= room, owner * rest + before - room, -1)
    place = (target[:, None] == jnp.arange(host_count * rest)[None, :]).astype(jnp.float32)
    number = (adapter % owned_total + 1).astype(jnp.float32)
    numbers = jnp.broadcast_to((place.T @ number)[:, None], (host_count * rest, LANES))
    rows = jnp.dot(
        place.T.astype(jnp.bfloat16), attended, preferred_element_type=jnp.float32
    ).astype(jnp.bfloat16)
    rows = jnp.concatenate([rows, numbers.astype(jnp.bfloat16)], axis=1)
    rows = lax.all_to_all(rows, "hst", split_axis=0, concat_axis=0, tiled=True)
    number = rows[:, feature_here].astype(jnp.int32)
    rows = rows[:, :feature_here]
    uses = number[:, None] == jnp.arange(1, owned_total + 1)[None, :]
    product = jnp.einsum("rd,akd->rak", rows, down, preferred_element_type=jnp.float32)
    partial_sum = jnp.sum(jnp.where(uses[:, :, None], product, 0), axis=1)
    shrunk = sum([partial_sum] + [swap(partial_sum, "tp", k) for k in range(1, tp_count)])
    spread = jnp.where(uses[:, :, None], shrunk.astype(jnp.bfloat16)[:, None, :], 0)
    raised = jnp.einsum("rak,aki->ri", spread, up, preferred_element_type=jnp.float32)
    back = lax.all_to_all(
        raised.astype(jnp.bfloat16), "hst", split_axis=0, concat_axis=0, tiled=True
    )
    return jnp.dot(place.astype(jnp.bfloat16), back, preferred_element_type=jnp.float32)


def local(
    queries,
    key_page_cache,
    value_page_cache,
    request_pages,
    context_length,
    output_weight,
    adapter_down_weight,
    adapter_up_weight,
    residual,
    host_slot_adapter,
    request_slot,
):
    owned_total, rank, feature_here = adapter_down_weight.shape
    host_count = lax.axis_size("hst")
    tp_count = lax.axis_size("tp")
    slot_total = host_slot_adapter.shape[0]
    most = pair_rows(slot_total, host_count)
    room = min(FIRST, most)
    (attended, place, down), evens, odd, blocks = attend(
        queries,
        key_page_cache,
        value_page_cache,
        request_pages.T,
        context_length,
        request_slot.reshape(1, -1),
        host_slot_adapter.reshape(1, slot_total),
        adapter_down_weight.reshape(owned_total * rank, feature_here),
        output_weight,
        owned_total,
        host_count,
        room,
    )
    near = swap(odd, "tp", 1)
    row_count = attended.shape[0]
    bases = [evens[0], near]
    for k in range(2, tp_count, 2):
        pair = evens[k // 2] + near[k // 2 * row_count : (k // 2 + 1) * row_count]
        bases.append(swap(pair, "tp", k))
    blocks = swap_all(blocks, "hst")
    partial_sum, number, over, up = shrink(
        blocks, down, adapter_up_weight.reshape(owned_total * rank, -1), room
    )
    parts = swap_all([partial_sum] * tp_count, "tp")
    parts, bases = lax.optimization_barrier((parts, bases))
    raised = expand(parts, number, up, host_count)
    backs = swap_all(raised, "hst")
    if room == most:
        return finish(place, residual, bases, backs)

    def with_second(bases, backs):
        more = second_pass(
            attended,
            adapter_down_weight,
            adapter_up_weight,
            host_slot_adapter,
            request_slot[:, 0],
            room,
            up_to(most - room, 16),
        )
        return finish(place, residual, bases, backs, more)

    def first_only(bases, backs):
        return finish(place, residual, bases, backs)

    return lax.cond(over[0] > 0, with_second, first_only, bases, backs)


def solution(mesh):
    in_specs = (
        P("hst", "tp"),
        P("hst", None, "tp"),
        P("hst", None, "tp"),
        P("hst", None),
        P("hst"),
        P("tp", None),
        P("hst", None, "tp"),
        P("hst", None, "tp"),
        P("hst", "tp"),
        P("hst"),
        P("hst", None),
    )
    out_specs = P("hst", "tp")
    return jax.shard_map(local, mesh=mesh, in_specs=in_specs, out_specs=out_specs, check_vma=False)
```

```python
import functools
import math

import jax
import jax.numpy as jnp
from jax import lax
from jax.experimental import pallas as pl
from jax.experimental.pallas import tpu as pltpu
from jax.sharding import PartitionSpec as P

HD = 128
LANES = 128
HEAD_ROWS = 8
GROUP = 16
ADAPTER_SCALE = 2.0
CAP = 4
FIRST = 20
CHUNKS = 4

MIB = 1 << 20
NT = (((1,), (1,)), ((), ()))
TN = (((0,), (0,)), ((), ()))
NN = (((1,), (0,)), ((), ()))


def iota(shape, axis):
    return lax.broadcasted_iota(jnp.int32, shape, axis)


def pair_rows(slot_total, host_count):
    return CAP * (2 * slot_total // host_count)


def up_to(value, step):
    return -(-value // step) * step


def block_of(k, count):
    return jnp.where(k == 0, 0, count - k)


def partners(count):
    return [0, *range(count - 1, 0, -1)]


def copies(source, target, sem, count):
    cut = source.shape[0] // count
    return [
        pltpu.make_async_copy(
            source.at[pl.ds(i * cut, cut)], target.at[pl.ds(i * cut, cut)], sem.at[i]
        )
        for i in range(count)
    ]


def in_hbm(*arrays):
    return [pltpu.with_memory_space_constraint(a, pltpu.HBM) for a in arrays]


def attention_kernel(owned_total, host_count, room, *refs):
    pages_hbm, length_hbm, query_hbm, slot_hbm, stock_hbm, keys_hbm, values_hbm = refs[:7]
    down_hbm, up_hbm, attended_ref, place_ref, down_ref, up_ref = refs[7:13]
    block_refs, refs = refs[13 : 13 + host_count], refs[13 + host_count :]
    (
        pages_ref,
        length_ref,
        query_ref,
        slot_ref,
        stock_ref,
        keys,
        values,
        query_rows,
        outcome,
        packed,
        numbers,
        counts,
        small_sem,
        key_sem,
        value_sem,
        weight_sem,
    ) = refs
    row_count, feature_here = query_ref.shape
    page_total, page, kv_width = keys_hbm.shape
    heads = feature_here // HD
    kv_here = kv_width // HD
    share = heads // kv_here
    most_pages = pages_ref.shape[0]
    context = most_pages * page

    small_moves = [
        pltpu.make_async_copy(source, target, small_sem.at[i])
        for i, (source, target) in enumerate(
            (
                (query_hbm, query_ref),
                (slot_hbm, slot_ref),
                (stock_hbm, stock_ref),
                (pages_hbm, pages_ref),
                (length_hbm, length_ref),
            )
        )
    ]
    key_moves = copies(keys_hbm, keys, key_sem, CHUNKS)
    value_moves = copies(values_hbm, values, value_sem, CHUNKS)
    weight_moves = copies(down_hbm, down_ref, weight_sem.at[0], CHUNKS)
    weight_moves += copies(up_hbm, up_ref, weight_sem.at[1], CHUNKS)
    for move in small_moves + key_moves + value_moves:
        move.start()
    packed[...] = jnp.zeros_like(packed)
    numbers[...] = jnp.zeros_like(numbers)
    for o in range(host_count):
        counts[o] = 0
    for move in small_moves:
        move.wait()

    if heads < HEAD_ROWS:
        query_rows[...] = jnp.zeros_like(query_rows)
    for j in range(heads):
        query_rows[pl.ds(j, row_count, stride=HEAD_ROWS), :] = query_ref[
            :, j * HD : (j + 1) * HD
        ].astype(jnp.float32)

    me = lax.axis_index("hst")
    pad = up_to(room, 8)

    def count(r, most):
        adapter = stock_ref[0, slot_ref[0, r]]
        owner = lax.div(adapter, owned_total)
        before = counts[owner]
        counts[owner] = before + 1
        block = block_of(owner ^ me, host_count)
        fits = before < room
        place_ref[r] = jnp.where(fits, block * room + before, host_count * room)
        where = jnp.where(fits, block * pad + before, host_count * pad)
        number = jnp.full((1, LANES), adapter - owner * owned_total + 1, jnp.int32)
        numbers[pl.ds(where, 1), :] = number.astype(jnp.float32)
        return jnp.maximum(most, before)

    most = lax.fori_loop(0, row_count, count, jnp.int32(0))
    over = jnp.where(jnp.full((8, LANES), most, jnp.int32) >= room, 1.0, 0.0)

    for move in key_moves:
        move.wait()
    for move in weight_moves:
        move.start()

    head_of = iota((HEAD_ROWS, HD), 0) // share

    def tile_of(r):
        return pl.ds(pl.multiple_of(r * HEAD_ROWS, HEAD_ROWS), HEAD_ROWS)

    def some_scores(step, carry):
        first = step * GROUP
        scores = []
        for i in range(GROUP):
            r = first + i
            rows = query_rows[tile_of(r), :]
            wide = jnp.concatenate(
                [jnp.where(head_of == c, rows, 0.0) for c in range(kv_here)], axis=1
            ).astype(jnp.bfloat16)
            held = jnp.concatenate([keys[pages_ref[p, r]] for p in range(most_pages)], axis=0)
            part = lax.dot_general(wide, held, NT, preferred_element_type=jnp.float32)
            live = iota((HEAD_ROWS, context), 1) < length_ref[r]
            scores.append(jnp.where(live, part * (1.0 / math.sqrt(HD)), -jnp.inf))
        score = jnp.concatenate(scores, axis=0)
        weight = jnp.exp(score - jnp.max(score, axis=1, keepdims=True))
        weight = weight / jnp.sum(weight, axis=1, keepdims=True)
        size = GROUP * HEAD_ROWS
        outcome[pl.ds(pl.multiple_of(step * size, size), size), :] = weight
        return carry

    def some_values(step, carry):
        first = step * GROUP
        for i in range(GROUP):
            r = first + i
            held = jnp.concatenate([values[pages_ref[p, r]] for p in range(most_pages)], axis=0)
            part = lax.dot_general(
                outcome[tile_of(r), :].astype(jnp.bfloat16),
                held,
                NN,
                preferred_element_type=jnp.float32,
            )
            result = part[:, :HD]
            for c in range(1, kv_here):
                result = jnp.where(head_of == c, part[:, c * HD : (c + 1) * HD], result)
            outcome[tile_of(r), :] = result
            packed[tile_of(place_ref[r]), :] = result
        return carry

    lax.fori_loop(0, row_count // GROUP, some_scores, 0)
    for move in value_moves:
        move.wait()
    lax.fori_loop(0, row_count // GROUP, some_values, 0)

    lane = iota((8, LANES), 1)
    size = room * HEAD_ROWS
    for k in range(host_count):
        tile = jnp.where(lane == LANES - 1, over, 0.0)
        for b in range(pad // 8):
            tile = jnp.where(lane == b, numbers[k * pad + 8 * b : k * pad + 8 * b + 8], tile)
        block_refs[k][...] = jnp.concatenate(
            [packed[k * size : (k + 1) * size], tile], axis=0
        ).astype(jnp.bfloat16)
    for j in range(heads):
        attended_ref[:, j * HD : (j + 1) * HD] = outcome[
            pl.ds(j, row_count, stride=HEAD_ROWS), :
        ].astype(jnp.bfloat16)
    for move in weight_moves:
        move.wait()


def attend(
    queries, keys, values, pages, lengths, slots, stock, down, up, owned_total, hosts, room
):
    row_count, feature_here = queries.shape
    spec = pl.BlockSpec(memory_space=pltpu.VMEM)
    small = pl.BlockSpec(memory_space=pltpu.SMEM)
    far = pl.BlockSpec(memory_space=pl.ANY)
    block = jax.ShapeDtypeStruct((room * HEAD_ROWS + 8, LANES), jnp.bfloat16)
    outs = pl.pallas_call(
        functools.partial(attention_kernel, owned_total, hosts, room),
        name="attend",
        out_shape=[
            jax.ShapeDtypeStruct((row_count, feature_here), jnp.bfloat16),
            jax.ShapeDtypeStruct((row_count,), jnp.int32),
            pltpu.VMEM(down.shape, jnp.bfloat16),
            pltpu.VMEM(up.shape, jnp.bfloat16),
        ]
        + [block] * hosts,
        in_specs=[far] * 9,
        out_specs=[spec, small, spec, spec] + [spec] * hosts,
        scratch_shapes=[
            pltpu.SMEM(pages.shape, jnp.int32),
            pltpu.SMEM(lengths.shape, jnp.int32),
            pltpu.VMEM(queries.shape, jnp.bfloat16),
            pltpu.SMEM(slots.shape, jnp.int32),
            pltpu.SMEM(stock.shape, jnp.int32),
            pltpu.VMEM(keys.shape, jnp.bfloat16),
            pltpu.VMEM(values.shape, jnp.bfloat16),
            pltpu.VMEM((row_count * HEAD_ROWS, HD), jnp.float32),
            pltpu.VMEM((row_count * HEAD_ROWS, HD), jnp.float32),
            pltpu.VMEM(((hosts * room + 1) * HEAD_ROWS, HD), jnp.float32),
            pltpu.VMEM((hosts * up_to(room, 8) + 8, LANES), jnp.float32),
            pltpu.SMEM((hosts,), jnp.int32),
            pltpu.SemaphoreType.DMA((5,)),
            pltpu.SemaphoreType.DMA((CHUNKS,)),
            pltpu.SemaphoreType.DMA((CHUNKS,)),
            pltpu.SemaphoreType.DMA((2, CHUNKS)),
        ],
        compiler_params=pltpu.CompilerParams(vmem_limit_bytes=24 * MIB),
        cost_estimate=pl.CostEstimate(
            flops=4 * row_count * HEAD_ROWS * 128 * feature_here,
            bytes_accessed=4 * keys.size + 4 * down.size,
            transcendentals=row_count * HEAD_ROWS * 128,
        ),
    )(*in_hbm(pages, lengths, queries, slots, stock, keys, values, down, up))
    return outs[:4], outs[4:]


def base_moves(weight_hbm, weight, sem, parity):
    count, parts = sem.shape
    me = lax.axis_index("tp")
    depth, width = weight.shape[1:]
    cut = depth // parts
    moves = []
    for i in range(count):
        columns = pl.ds(pl.multiple_of((me ^ (2 * i + parity)) * width, width), width)
        for part in range(parts):
            rows = pl.ds(part * cut, cut)
            moves.append(
                pltpu.make_async_copy(
                    weight_hbm.at[rows, columns], weight.at[i, rows], sem.at[i, part]
                )
            )
    return moves


def odd_kernel(attended_ref, weight_hbm, out_ref, weight, sem):
    moves = base_moves(weight_hbm, weight, sem, 1)
    for move in moves:
        move.start()
    count, parts = sem.shape
    rows = attended_ref[...]
    for i in range(count):
        for move in moves[i * parts : (i + 1) * parts]:
            move.wait()
        out_ref[i * rows.shape[0] : (i + 1) * rows.shape[0]] = jnp.dot(
            rows, weight[i], preferred_element_type=jnp.float32
        ).astype(jnp.bfloat16)


def even_kernel(attended_ref, weight_hbm, *refs):
    outs, (weight, sem) = refs[:-2], refs[-2:]
    moves = base_moves(weight_hbm, weight, sem, 0)
    for move in moves:
        move.start()
    count, parts = sem.shape
    rows = attended_ref[...]
    for i in range(count):
        for move in moves[i * parts : (i + 1) * parts]:
            move.wait()
        outs[i][...] = jnp.dot(rows, weight[i], preferred_element_type=jnp.float32).astype(
            jnp.bfloat16
        )


def base_half(kernel, name, attended, weight, out_shape):
    row_count, depth = attended.shape
    count = weight.shape[1] // depth // 2
    spec = pl.BlockSpec(memory_space=pltpu.VMEM)
    return pl.pallas_call(
        kernel,
        name=name,
        out_shape=out_shape,
        in_specs=[spec, pl.BlockSpec(memory_space=pl.ANY)],
        out_specs=jax.tree.map(lambda _: spec, out_shape),
        scratch_shapes=[
            pltpu.VMEM((count, depth, depth), jnp.bfloat16),
            pltpu.SemaphoreType.DMA((count, 8)),
        ],
        compiler_params=pltpu.CompilerParams(vmem_limit_bytes=12 * MIB),
        cost_estimate=pl.CostEstimate(
            flops=row_count * weight.size, bytes_accessed=weight.size, transcendentals=0
        ),
    )(attended, *in_hbm(weight))


def shrink_kernel(host_count, room, *refs):
    blocks = refs[:host_count]
    down_ref, odd_ref, partial_ref, joint_ref, number_ref, over_ref = refs[host_count:-2]
    tiles, total = refs[-2:]
    heads = down_ref.shape[1] // HD
    rows_all = host_count * room
    size = room * HEAD_ROWS
    width = 256
    rank = LANES // 2
    over = jnp.float32(0)
    lane = iota((8, LANES), 1)
    for k in range(host_count):
        tiles[k * size : (k + 1) * size] = blocks[k][:size].astype(jnp.float32)
        tile = blocks[k][size:].astype(jnp.float32)
        over = jnp.maximum(over, jnp.max(jnp.where(lane == LANES - 1, tile, 0.0)))
        for b in range(up_to(room, 8) // 8):
            rest = min(8, room - 8 * b)
            column = jnp.sum(jnp.where(lane == b, tile, 0.0), axis=1, keepdims=True)
            column = jnp.broadcast_to(column, (8, LANES))
            number_ref[k * room + 8 * b : k * room + 8 * b + rest] = column[:rest]
    over_ref[0] = (over > 0).astype(jnp.int32)
    rows = jnp.concatenate(
        [tiles[pl.ds(j, rows_all, stride=HEAD_ROWS), :].astype(jnp.bfloat16) for j in range(heads)],
        axis=1,
    )
    number = number_ref[...]
    own = (iota(number.shape, 1) // rank).astype(jnp.float32) + 1.0
    for step in range(down_ref.shape[0] // width):
        product = lax.dot_general(
            rows,
            down_ref[step * width : (step + 1) * width],
            NT,
            preferred_element_type=jnp.float32,
        )
        add = jnp.zeros_like(number) if step == 0 else total[...]
        for i in range(width // LANES):
            piece = product[:, i * LANES : (i + 1) * LANES]
            first = 2.0 * (step * (width // LANES) + i)
            add = jnp.where(number == own + first, piece + add, add)
        total[...] = add
    full = total[...]
    full = full + pltpu.roll(full, rank, 1)
    half = rows_all // 2
    left = iota((half, LANES), 1) < rank
    partial_ref[...] = jnp.where(left, full[:half], full[half:]).astype(jnp.bfloat16)
    joint_ref[:half] = partial_ref[...]
    odd_rows = odd_ref.shape[0]
    for j in range(odd_ref.shape[1] // LANES):
        first = half + j * odd_rows
        joint_ref[first : first + odd_rows] = odd_ref[:, j * LANES : (j + 1) * LANES]


def shrink(blocks, down, odd, room):
    host_count = len(blocks)
    rows = host_count * room
    spec = pl.BlockSpec(memory_space=pltpu.VMEM)
    return pl.pallas_call(
        functools.partial(shrink_kernel, host_count, room),
        name="shrink",
        out_shape=(
            jax.ShapeDtypeStruct((rows // 2, LANES), jnp.bfloat16),
            jax.ShapeDtypeStruct((rows // 2 + odd.size // LANES, LANES), jnp.bfloat16),
            jax.ShapeDtypeStruct((rows, LANES), jnp.float32),
            jax.ShapeDtypeStruct((1,), jnp.int32),
        ),
        in_specs=[spec] * (host_count + 2),
        out_specs=(spec, spec, spec, pl.BlockSpec(memory_space=pltpu.SMEM)),
        scratch_shapes=[
            pltpu.VMEM((rows * HEAD_ROWS, HD), jnp.float32),
            pltpu.VMEM((rows, LANES), jnp.float32),
        ],
        compiler_params=pltpu.CompilerParams(vmem_limit_bytes=12 * MIB),
        cost_estimate=pl.CostEstimate(
            flops=2 * rows * down.size, bytes_accessed=2 * down.size, transcendentals=0
        ),
    )(*blocks, down, odd)


def expand_kernel(part_count, even_count, host_count, *refs):
    parts, refs = refs[:part_count], refs[part_count:]
    evens, (number_ref, up_ref), refs = refs[:even_count], refs[even_count:][:2], refs[even_count + 2 :]
    outs, sums, (spread, tiles) = refs[:host_count], refs[host_count:-2], refs[-2:]
    rows, columns = number_ref.shape[0], up_ref.shape[1]
    width = min(256, columns)
    rank = LANES // 2
    half = rows // 2
    full = parts[0][...].astype(jnp.float32)
    for p in parts[1:]:
        full = full + p[:half].astype(jnp.float32)
    other = pltpu.roll(full, rank, 1)
    left = iota(full.shape, 1) < rank
    both = jnp.concatenate(
        [jnp.where(left, full, other), jnp.where(left, other, full)], axis=0
    )
    number = number_ref[...]
    own = (iota(number.shape, 1) // rank).astype(jnp.float32) + 1.0
    for i in range(spread.shape[1] // LANES):
        spread[:, i * LANES : (i + 1) * LANES] = jnp.where(
            number == own + 2.0 * i, both, 0.0
        ).astype(jnp.bfloat16)
    if columns // HD < HEAD_ROWS:
        tiles[...] = jnp.zeros_like(tiles)
    for i in range(columns // width):
        result = jnp.dot(
            spread[...],
            up_ref[:, i * width : (i + 1) * width],
            preferred_element_type=jnp.float32,
        )
        for j in range(width // HD):
            tiles[pl.ds(i * (width // HD) + j, rows, stride=HEAD_ROWS), :] = result[
                :, j * HD : (j + 1) * HD
            ]
    size = rows // host_count * HEAD_ROWS
    for k in range(host_count):
        outs[k][...] = tiles[k * size : (k + 1) * size].astype(jnp.bfloat16)
    row_count = evens[0].shape[0]
    for i in range(even_count):
        for j in range(columns // LANES):
            first = half + (j * even_count + i) * row_count
            cut = slice(j * LANES, (j + 1) * LANES)
            sums[i][:, cut] = (
                evens[i][:, cut].astype(jnp.float32)
                + parts[1][first : first + row_count].astype(jnp.float32)
            ).astype(jnp.bfloat16)


def expand(parts, evens, number, up, host_count):
    rows = number.shape[0]
    depth, columns = up.shape
    spec = pl.BlockSpec(memory_space=pltpu.VMEM)
    block = jax.ShapeDtypeStruct((rows // host_count * HEAD_ROWS, HD), jnp.bfloat16)
    outs = pl.pallas_call(
        functools.partial(expand_kernel, len(parts), len(evens), host_count),
        name="expand",
        out_shape=[block] * host_count
        + [jax.ShapeDtypeStruct(e.shape, jnp.bfloat16) for e in evens],
        in_specs=[spec] * (len(parts) + len(evens) + 2),
        out_specs=[spec] * (host_count + len(evens)),
        scratch_shapes=[
            pltpu.VMEM((rows, depth), jnp.bfloat16),
            pltpu.VMEM((rows * HEAD_ROWS, HD), jnp.float32),
        ],
        compiler_params=pltpu.CompilerParams(vmem_limit_bytes=12 * MIB),
        cost_estimate=pl.CostEstimate(
            flops=2 * rows * up.size, bytes_accessed=2 * up.size, transcendentals=0
        ),
    )(*parts, *evens, number, up)
    return outs[:host_count], outs[host_count:]


def finish_kernel(base_count, back_count, place_ref, residual_ref, *refs):
    bases, backs = refs[:base_count], refs[base_count : base_count + back_count]
    more, (out_ref, tiles, sorted_tiles) = refs[base_count + back_count : -3], refs[-3:]
    row_count, columns = residual_ref.shape
    size = backs[0].shape[0]
    for k in range(back_count):
        tiles[k * size : (k + 1) * size] = backs[k][...].astype(jnp.float32)
    tiles[back_count * size :] = jnp.zeros((HEAD_ROWS, HD), jnp.float32)
    for r in range(row_count):
        where = pl.multiple_of(place_ref[r] * HEAD_ROWS, HEAD_ROWS)
        sorted_tiles[r * HEAD_ROWS : (r + 1) * HEAD_ROWS] = tiles[pl.ds(where, HEAD_ROWS), :]
    for j in range(columns // HD):
        cut = slice(j * HD, (j + 1) * HD)
        total = sorted_tiles[pl.ds(j, row_count, stride=HEAD_ROWS), :]
        for m in more:
            total = total + m[:, cut]
        total = residual_ref[:, cut].astype(jnp.float32) + ADAPTER_SCALE * total
        for b in bases:
            total = total + b[:, cut].astype(jnp.float32)
        out_ref[:, cut] = total.astype(jnp.bfloat16)


def finish(place, residual, bases, backs, *more):
    spec = pl.BlockSpec(memory_space=pltpu.VMEM)
    size = backs[0].shape[0]
    return pl.pallas_call(
        functools.partial(finish_kernel, len(bases), len(backs)),
        name="finish",
        out_shape=pltpu.HBM(residual.shape, jnp.bfloat16),
        in_specs=[pl.BlockSpec(memory_space=pltpu.SMEM)]
        + [spec] * (1 + len(bases) + len(backs) + len(more)),
        out_specs=spec,
        scratch_shapes=[
            pltpu.VMEM((len(backs) * size + HEAD_ROWS, HD), jnp.float32),
            pltpu.VMEM((residual.shape[0] * HEAD_ROWS, HD), jnp.float32),
        ],
        compiler_params=pltpu.CompilerParams(vmem_limit_bytes=8 * MIB),
    )(place, residual, *bases, *backs, *more)


def swap(value, axis, k):
    size = lax.axis_size(axis)
    return lax.ppermute(value, axis, [(i, i ^ k) for i in range(size)])


def swap_all(values, axis, ks):
    return [v if k == 0 else swap(v, axis, k) for v, k in zip(values, ks)]


def second_pass(attended, down, up, stock, slots, room, rest):
    owned_total, rank, feature_here = down.shape
    host_count = lax.axis_size("hst")
    tp_count = lax.axis_size("tp")
    row_count = attended.shape[0]
    adapter = stock[slots]
    owner = adapter // owned_total
    order = jnp.arange(row_count)
    same = (owner[:, None] == owner[None, :]) & (order[None, :] < order[:, None])
    before = jnp.sum(same, axis=1)
    target = jnp.where(before >= room, owner * rest + before - room, -1)
    place = (target[:, None] == jnp.arange(host_count * rest)[None, :]).astype(jnp.float32)
    number = (adapter % owned_total + 1).astype(jnp.float32)
    numbers = jnp.broadcast_to((place.T @ number)[:, None], (host_count * rest, LANES))
    rows = jnp.dot(
        place.T.astype(jnp.bfloat16), attended, preferred_element_type=jnp.float32
    ).astype(jnp.bfloat16)
    rows = jnp.concatenate([rows, numbers.astype(jnp.bfloat16)], axis=1)
    rows = lax.all_to_all(rows, "hst", split_axis=0, concat_axis=0, tiled=True)
    number = rows[:, feature_here].astype(jnp.int32)
    rows = rows[:, :feature_here]
    uses = number[:, None] == jnp.arange(1, owned_total + 1)[None, :]
    product = jnp.einsum("rd,akd->rak", rows, down, preferred_element_type=jnp.float32)
    partial_sum = jnp.sum(jnp.where(uses[:, :, None], product, 0), axis=1)
    shrunk = sum([partial_sum] + [swap(partial_sum, "tp", k) for k in range(1, tp_count)])
    spread = jnp.where(uses[:, :, None], shrunk.astype(jnp.bfloat16)[:, None, :], 0)
    raised = jnp.einsum("rak,aki->ri", spread, up, preferred_element_type=jnp.float32)
    back = lax.all_to_all(
        raised.astype(jnp.bfloat16), "hst", split_axis=0, concat_axis=0, tiled=True
    )
    return jnp.dot(place.astype(jnp.bfloat16), back, preferred_element_type=jnp.float32)


def local(
    queries,
    key_page_cache,
    value_page_cache,
    request_pages,
    context_length,
    output_weight,
    adapter_down_weight,
    adapter_up_weight,
    residual,
    host_slot_adapter,
    request_slot,
):
    owned_total, rank, feature_here = adapter_down_weight.shape
    host_count = lax.axis_size("hst")
    tp_count = lax.axis_size("tp")
    slot_total = host_slot_adapter.shape[0]
    most = pair_rows(slot_total, host_count)
    room = min(FIRST, most)
    (attended, place, down, up), blocks = attend(
        queries,
        key_page_cache,
        value_page_cache,
        request_pages.T,
        context_length,
        request_slot.reshape(1, -1),
        host_slot_adapter.reshape(1, slot_total),
        adapter_down_weight.reshape(owned_total * rank, feature_here),
        adapter_up_weight.reshape(owned_total * rank, -1),
        owned_total,
        host_count,
        room,
    )
    row_count = attended.shape[0]
    ks = partners(host_count)
    blocks = swap_all(blocks, "hst", ks)
    evens = tp_count // 2
    one = jax.ShapeDtypeStruct((row_count, feature_here), jnp.bfloat16)
    odd = jax.ShapeDtypeStruct((evens * row_count, feature_here), jnp.bfloat16)
    odd = base_half(odd_kernel, "base_odd", attended, output_weight, odd)
    blocks, odd = lax.optimization_barrier((blocks, odd))
    partial_sum, joint, number, over = shrink(blocks, down, odd, room)
    parts = [partial_sum, joint] + [partial_sum] * (tp_count - 2)
    parts = swap_all(parts, "tp", range(tp_count))
    even = base_half(even_kernel, "base_even", attended, output_weight, [one] * evens)
    parts, even = lax.optimization_barrier((parts, even))
    raised, bases = expand(parts, even, number, up, host_count)
    bases = swap_all(bases, "tp", range(0, tp_count, 2))
    late = host_count // 2 + 1
    last, bases = lax.optimization_barrier((raised[late:], bases))
    backs = swap_all([*raised[:late], *last], "hst", ks)
    if room == most:
        return finish(place, residual, bases, backs)

    def with_second(bases, backs):
        more = second_pass(
            attended,
            adapter_down_weight,
            adapter_up_weight,
            host_slot_adapter,
            request_slot[:, 0],
            room,
            up_to(most - room, 16),
        )
        return finish(place, residual, bases, backs, more)

    def first_only(bases, backs):
        return finish(place, residual, bases, backs)

    return lax.cond(over[0] > 0, with_second, first_only, bases, backs)


def solution(mesh):
    in_specs = (
        P("hst", "tp"),
        P("hst", None, "tp"),
        P("hst", None, "tp"),
        P("hst", None),
        P("hst"),
        P("tp", None),
        P("hst", None, "tp"),
        P("hst", None, "tp"),
        P("hst", "tp"),
        P("hst"),
        P("hst", None),
    )
    out_specs = P("hst", "tp")
    return jax.shard_map(local, mesh=mesh, in_specs=in_specs, out_specs=out_specs, check_vma=False)
```

```python
import functools
import math

import jax
import jax.numpy as jnp
from jax import lax
from jax.experimental import pallas as pl
from jax.experimental.pallas import tpu as pltpu
from jax.sharding import PartitionSpec as P

HD = 128
LANES = 128
HEAD_ROWS = 8
GROUP = 16
ADAPTER_SCALE = 2.0
CAP = 4
FIRST = 20
CHUNKS = 8

MIB = 1 << 20
NT = (((1,), (1,)), ((), ()))
TN = (((0,), (0,)), ((), ()))
NN = (((1,), (0,)), ((), ()))


def iota(shape, axis):
    return lax.broadcasted_iota(jnp.int32, shape, axis)


def pair_rows(slot_total, host_count):
    return CAP * (2 * slot_total // host_count)


def up_to(value, step):
    return -(-value // step) * step


def block_of(k, count):
    return jnp.where(k == 0, 0, count - k)


def partners(count):
    return [0, *range(count - 1, 0, -1)]


def copies(source, target, sem, count):
    cut = source.shape[0] // count
    return [
        pltpu.make_async_copy(
            source.at[pl.ds(i * cut, cut)], target.at[pl.ds(i * cut, cut)], sem.at[i]
        )
        for i in range(count)
    ]


def in_hbm(*arrays):
    return [pltpu.with_memory_space_constraint(a, pltpu.HBM) for a in arrays]


def attention_kernel(owned_total, host_count, room, *refs):
    pages_hbm, length_hbm, query_hbm, slot_hbm, stock_hbm, keys_hbm, values_hbm = refs[:7]
    down_hbm, attended_ref, place_ref, down_ref = refs[7:11]
    block_refs, refs = refs[11 : 11 + host_count], refs[11 + host_count :]
    (
        pages_ref,
        length_ref,
        query_ref,
        slot_ref,
        stock_ref,
        keys,
        values,
        query_rows,
        outcome,
        packed,
        numbers,
        counts,
        small_sem,
        key_sem,
        value_sem,
        weight_sem,
    ) = refs
    row_count, feature_here = query_ref.shape
    page_total, page, kv_width = keys_hbm.shape
    heads = feature_here // HD
    kv_here = kv_width // HD
    share = heads // kv_here
    most_pages = pages_ref.shape[0]
    context = most_pages * page

    small_moves = [
        pltpu.make_async_copy(source, target, small_sem.at[i])
        for i, (source, target) in enumerate(
            (
                (query_hbm, query_ref),
                (slot_hbm, slot_ref),
                (stock_hbm, stock_ref),
                (pages_hbm, pages_ref),
                (length_hbm, length_ref),
            )
        )
    ]
    key_moves = copies(keys_hbm, keys, key_sem, CHUNKS)
    value_moves = copies(values_hbm, values, value_sem, CHUNKS)
    weight_moves = copies(down_hbm, down_ref, weight_sem, CHUNKS)
    for move in small_moves + key_moves:
        move.start()
    packed[...] = jnp.zeros_like(packed)
    numbers[...] = jnp.zeros_like(numbers)
    for o in range(host_count):
        counts[o] = 0
    for move in small_moves:
        move.wait()
    for move in value_moves:
        move.start()

    if heads < HEAD_ROWS:
        query_rows[...] = jnp.zeros_like(query_rows)
    for j in range(heads):
        query_rows[pl.ds(j, row_count, stride=HEAD_ROWS), :] = query_ref[
            :, j * HD : (j + 1) * HD
        ].astype(jnp.float32)

    me = lax.axis_index("hst")
    pad = up_to(room, 8)

    def count(r, most):
        adapter = stock_ref[0, slot_ref[0, r]]
        owner = lax.div(adapter, owned_total)
        before = counts[owner]
        counts[owner] = before + 1
        block = block_of(owner ^ me, host_count)
        fits = before < room
        place_ref[r] = jnp.where(fits, block * room + before, host_count * room)
        where = jnp.where(fits, block * pad + before, host_count * pad)
        number = jnp.full((1, LANES), adapter - owner * owned_total + 1, jnp.int32)
        numbers[pl.ds(where, 1), :] = number.astype(jnp.float32)
        return jnp.maximum(most, before)

    most = lax.fori_loop(0, row_count, count, jnp.int32(0))
    over = jnp.where(jnp.full((8, LANES), most, jnp.int32) >= room, 1.0, 0.0)

    for move in key_moves:
        move.wait()
    for move in weight_moves:
        move.start()

    head_of = iota((HEAD_ROWS, HD), 0) // share

    def tile_of(r):
        return pl.ds(pl.multiple_of(r * HEAD_ROWS, HEAD_ROWS), HEAD_ROWS)

    def some_scores(step, carry):
        first = step * GROUP
        scores = []
        for i in range(GROUP):
            r = first + i
            rows = query_rows[tile_of(r), :]
            wide = jnp.concatenate(
                [jnp.where(head_of == c, rows, 0.0) for c in range(kv_here)], axis=1
            ).astype(jnp.bfloat16)
            held = jnp.concatenate([keys[pages_ref[p, r]] for p in range(most_pages)], axis=0)
            part = lax.dot_general(wide, held, NT, preferred_element_type=jnp.float32)
            live = iota((HEAD_ROWS, context), 1) < length_ref[r]
            scores.append(jnp.where(live, part * (1.0 / math.sqrt(HD)), -jnp.inf))
        score = jnp.concatenate(scores, axis=0)
        weight = jnp.exp(score - jnp.max(score, axis=1, keepdims=True))
        weight = weight / jnp.sum(weight, axis=1, keepdims=True)
        size = GROUP * HEAD_ROWS
        outcome[pl.ds(pl.multiple_of(step * size, size), size), :] = weight
        return carry

    def some_values(step, carry):
        first = step * GROUP
        for i in range(GROUP):
            r = first + i
            held = jnp.concatenate([values[pages_ref[p, r]] for p in range(most_pages)], axis=0)
            part = lax.dot_general(
                outcome[tile_of(r), :].astype(jnp.bfloat16),
                held,
                NN,
                preferred_element_type=jnp.float32,
            )
            result = part[:, :HD]
            for c in range(1, kv_here):
                result = jnp.where(head_of == c, part[:, c * HD : (c + 1) * HD], result)
            outcome[tile_of(r), :] = result
            packed[tile_of(place_ref[r]), :] = result
        return carry

    lax.fori_loop(0, row_count // GROUP, some_scores, 0)
    for move in value_moves:
        move.wait()
    lax.fori_loop(0, row_count // GROUP, some_values, 0)

    lane = iota((8, LANES), 1)
    size = room * HEAD_ROWS
    for k in range(host_count):
        tile = jnp.where(lane == LANES - 1, over, 0.0)
        for b in range(pad // 8):
            tile = jnp.where(lane == b, numbers[k * pad + 8 * b : k * pad + 8 * b + 8], tile)
        block_refs[k][...] = jnp.concatenate(
            [packed[k * size : (k + 1) * size], tile], axis=0
        ).astype(jnp.bfloat16)
    for j in range(heads):
        attended_ref[:, j * HD : (j + 1) * HD] = outcome[
            pl.ds(j, row_count, stride=HEAD_ROWS), :
        ].astype(jnp.bfloat16)
    for move in weight_moves:
        move.wait()


def attend(
    queries, keys, values, pages, lengths, slots, stock, down, owned_total, hosts, room
):
    row_count, feature_here = queries.shape
    spec = pl.BlockSpec(memory_space=pltpu.VMEM)
    small = pl.BlockSpec(memory_space=pltpu.SMEM)
    far = pl.BlockSpec(memory_space=pl.ANY)
    block = jax.ShapeDtypeStruct((room * HEAD_ROWS + 8, LANES), jnp.bfloat16)
    outs = pl.pallas_call(
        functools.partial(attention_kernel, owned_total, hosts, room),
        name="attend",
        out_shape=[
            jax.ShapeDtypeStruct((row_count, feature_here), jnp.bfloat16),
            jax.ShapeDtypeStruct((row_count,), jnp.int32),
            pltpu.VMEM(down.shape, jnp.bfloat16),
        ]
        + [block] * hosts,
        in_specs=[far] * 8,
        out_specs=[spec, small, spec] + [spec] * hosts,
        scratch_shapes=[
            pltpu.SMEM(pages.shape, jnp.int32),
            pltpu.SMEM(lengths.shape, jnp.int32),
            pltpu.VMEM(queries.shape, jnp.bfloat16),
            pltpu.SMEM(slots.shape, jnp.int32),
            pltpu.SMEM(stock.shape, jnp.int32),
            pltpu.VMEM(keys.shape, jnp.bfloat16),
            pltpu.VMEM(values.shape, jnp.bfloat16),
            pltpu.VMEM((row_count * HEAD_ROWS, HD), jnp.float32),
            pltpu.VMEM((row_count * HEAD_ROWS, HD), jnp.float32),
            pltpu.VMEM(((hosts * room + 1) * HEAD_ROWS, HD), jnp.float32),
            pltpu.VMEM((hosts * up_to(room, 8) + 8, LANES), jnp.float32),
            pltpu.SMEM((hosts,), jnp.int32),
            pltpu.SemaphoreType.DMA((5,)),
            pltpu.SemaphoreType.DMA((CHUNKS,)),
            pltpu.SemaphoreType.DMA((CHUNKS,)),
            pltpu.SemaphoreType.DMA((CHUNKS,)),
        ],
        compiler_params=pltpu.CompilerParams(vmem_limit_bytes=24 * MIB),
        cost_estimate=pl.CostEstimate(
            flops=4 * row_count * HEAD_ROWS * 128 * feature_here,
            bytes_accessed=4 * keys.size + 2 * down.size,
            transcendentals=row_count * HEAD_ROWS * 128,
        ),
    )(*in_hbm(pages, lengths, queries, slots, stock, keys, values, down))
    return outs[:3], outs[3:]


def base_moves(weight_hbm, weight, sem, parity):
    count, parts = sem.shape
    me = lax.axis_index("tp")
    depth, width = weight.shape[1:]
    cut = depth // parts
    moves = []
    for i in range(count):
        columns = pl.ds(pl.multiple_of((me ^ (2 * i + parity)) * width, width), width)
        for part in range(parts):
            rows = pl.ds(part * cut, cut)
            moves.append(
                pltpu.make_async_copy(
                    weight_hbm.at[rows, columns], weight.at[i, rows], sem.at[i, part]
                )
            )
    return moves


def odd_kernel(attended_ref, weight_hbm, out_ref, weight, sem):
    moves = base_moves(weight_hbm, weight, sem, 1)
    for move in moves:
        move.start()
    count, parts = sem.shape
    rows = attended_ref[...]
    for i in range(count):
        for move in moves[i * parts : (i + 1) * parts]:
            move.wait()
        out_ref[i * rows.shape[0] : (i + 1) * rows.shape[0]] = jnp.dot(
            rows, weight[i], preferred_element_type=jnp.float32
        ).astype(jnp.bfloat16)


def even_kernel(attended_ref, weight_hbm, *refs):
    outs, (weight, sem) = refs[:-2], refs[-2:]
    moves = base_moves(weight_hbm, weight, sem, 0)
    for move in moves:
        move.start()
    count, parts = sem.shape
    rows = attended_ref[...]
    for i in range(count):
        for move in moves[i * parts : (i + 1) * parts]:
            move.wait()
        outs[i][...] = jnp.dot(rows, weight[i], preferred_element_type=jnp.float32).astype(
            jnp.bfloat16
        )


def base_half(kernel, name, attended, weight, out_shape):
    row_count, depth = attended.shape
    count = weight.shape[1] // depth // 2
    spec = pl.BlockSpec(memory_space=pltpu.VMEM)
    return pl.pallas_call(
        kernel,
        name=name,
        out_shape=out_shape,
        in_specs=[spec, pl.BlockSpec(memory_space=pl.ANY)],
        out_specs=jax.tree.map(lambda _: spec, out_shape),
        scratch_shapes=[
            pltpu.VMEM((count, depth, depth), jnp.bfloat16),
            pltpu.SemaphoreType.DMA((count, 8)),
        ],
        compiler_params=pltpu.CompilerParams(vmem_limit_bytes=12 * MIB),
        cost_estimate=pl.CostEstimate(
            flops=row_count * weight.size, bytes_accessed=weight.size, transcendentals=0
        ),
    )(attended, *in_hbm(weight))


def shrink_kernel(host_count, room, *refs):
    blocks = refs[:host_count]
    down_ref, odd_ref, up_hbm, partial_ref, joint_ref, number_ref, over_ref = refs[host_count:-4]
    up_ref, tiles, total, up_sem = refs[-4:]
    up_moves = copies(up_hbm, up_ref, up_sem, up_sem.shape[0])
    for move in up_moves:
        move.start()
    heads = down_ref.shape[1] // HD
    rows_all = host_count * room
    size = room * HEAD_ROWS
    width = 256
    rank = LANES // 2
    over = jnp.float32(0)
    lane = iota((8, LANES), 1)
    for k in range(host_count):
        tiles[k * size : (k + 1) * size] = blocks[k][:size].astype(jnp.float32)
        tile = blocks[k][size:].astype(jnp.float32)
        over = jnp.maximum(over, jnp.max(jnp.where(lane == LANES - 1, tile, 0.0)))
        for b in range(up_to(room, 8) // 8):
            rest = min(8, room - 8 * b)
            column = jnp.sum(jnp.where(lane == b, tile, 0.0), axis=1, keepdims=True)
            column = jnp.broadcast_to(column, (8, LANES))
            number_ref[k * room + 8 * b : k * room + 8 * b + rest] = column[:rest]
    over_ref[0] = (over > 0).astype(jnp.int32)
    rows = jnp.concatenate(
        [tiles[pl.ds(j, rows_all, stride=HEAD_ROWS), :].astype(jnp.bfloat16) for j in range(heads)],
        axis=1,
    )
    number = number_ref[...]
    own = (iota(number.shape, 1) // rank).astype(jnp.float32) + 1.0
    for step in range(down_ref.shape[0] // width):
        product = lax.dot_general(
            rows,
            down_ref[step * width : (step + 1) * width],
            NT,
            preferred_element_type=jnp.float32,
        )
        add = jnp.zeros_like(number) if step == 0 else total[...]
        for i in range(width // LANES):
            piece = product[:, i * LANES : (i + 1) * LANES]
            first = 2.0 * (step * (width // LANES) + i)
            add = jnp.where(number == own + first, piece + add, add)
        total[...] = add
    full = total[...]
    full = full + pltpu.roll(full, rank, 1)
    half = rows_all // 2
    left = iota((half, LANES), 1) < rank
    partial_ref[...] = jnp.where(left, full[:half], full[half:]).astype(jnp.bfloat16)
    joint_ref[:half] = partial_ref[...]
    odd_rows = odd_ref.shape[0]
    for j in range(odd_ref.shape[1] // LANES):
        first = half + j * odd_rows
        joint_ref[first : first + odd_rows] = odd_ref[:, j * LANES : (j + 1) * LANES]
    for move in up_moves:
        move.wait()


def shrink(blocks, down, odd, up, room):
    host_count = len(blocks)
    rows = host_count * room
    spec = pl.BlockSpec(memory_space=pltpu.VMEM)
    return pl.pallas_call(
        functools.partial(shrink_kernel, host_count, room),
        name="shrink",
        out_shape=(
            jax.ShapeDtypeStruct((rows // 2, LANES), jnp.bfloat16),
            jax.ShapeDtypeStruct((rows // 2 + odd.size // LANES, LANES), jnp.bfloat16),
            jax.ShapeDtypeStruct((rows, LANES), jnp.float32),
            jax.ShapeDtypeStruct((1,), jnp.int32),
            pltpu.VMEM(up.shape, jnp.bfloat16),
        ),
        in_specs=[spec] * (host_count + 2) + [pl.BlockSpec(memory_space=pl.ANY)],
        out_specs=(spec, spec, spec, pl.BlockSpec(memory_space=pltpu.SMEM), spec),
        scratch_shapes=[
            pltpu.VMEM((rows * HEAD_ROWS, HD), jnp.float32),
            pltpu.VMEM((rows, LANES), jnp.float32),
            pltpu.SemaphoreType.DMA((16,)),
        ],
        compiler_params=pltpu.CompilerParams(vmem_limit_bytes=12 * MIB),
        cost_estimate=pl.CostEstimate(
            flops=2 * rows * down.size, bytes_accessed=2 * down.size, transcendentals=0
        ),
    )(*blocks, down, odd, *in_hbm(up))


def expand_kernel(part_count, even_count, host_count, *refs):
    parts, refs = refs[:part_count], refs[part_count:]
    evens, (number_ref, up_ref), refs = refs[:even_count], refs[even_count:][:2], refs[even_count + 2 :]
    outs, sums, (spread, tiles) = refs[:host_count], refs[host_count:-2], refs[-2:]
    rows, columns = number_ref.shape[0], up_ref.shape[1]
    width = min(256, columns)
    rank = LANES // 2
    half = rows // 2
    full = parts[0][...].astype(jnp.float32)
    for p in parts[1:]:
        full = full + p[:half].astype(jnp.float32)
    other = pltpu.roll(full, rank, 1)
    left = iota(full.shape, 1) < rank
    both = jnp.concatenate(
        [jnp.where(left, full, other), jnp.where(left, other, full)], axis=0
    )
    number = number_ref[...]
    own = (iota(number.shape, 1) // rank).astype(jnp.float32) + 1.0
    for i in range(spread.shape[1] // LANES):
        spread[:, i * LANES : (i + 1) * LANES] = jnp.where(
            number == own + 2.0 * i, both, 0.0
        ).astype(jnp.bfloat16)
    if columns // HD < HEAD_ROWS:
        tiles[...] = jnp.zeros_like(tiles)
    for i in range(columns // width):
        result = jnp.dot(
            spread[...],
            up_ref[:, i * width : (i + 1) * width],
            preferred_element_type=jnp.float32,
        )
        for j in range(width // HD):
            tiles[pl.ds(i * (width // HD) + j, rows, stride=HEAD_ROWS), :] = result[
                :, j * HD : (j + 1) * HD
            ]
    size = rows // host_count * HEAD_ROWS
    for k in range(host_count):
        outs[k][...] = tiles[k * size : (k + 1) * size].astype(jnp.bfloat16)
    row_count = evens[0].shape[0]
    for i in range(even_count):
        for j in range(columns // LANES):
            first = half + (j * even_count + i) * row_count
            cut = slice(j * LANES, (j + 1) * LANES)
            sums[i][:, cut] = (
                evens[i][:, cut].astype(jnp.float32)
                + parts[1][first : first + row_count].astype(jnp.float32)
            ).astype(jnp.bfloat16)


def expand(parts, evens, number, up, host_count):
    rows = number.shape[0]
    depth, columns = up.shape
    spec = pl.BlockSpec(memory_space=pltpu.VMEM)
    block = jax.ShapeDtypeStruct((rows // host_count * HEAD_ROWS, HD), jnp.bfloat16)
    outs = pl.pallas_call(
        functools.partial(expand_kernel, len(parts), len(evens), host_count),
        name="expand",
        out_shape=[block] * host_count
        + [jax.ShapeDtypeStruct(e.shape, jnp.bfloat16) for e in evens],
        in_specs=[spec] * (len(parts) + len(evens) + 2),
        out_specs=[spec] * (host_count + len(evens)),
        scratch_shapes=[
            pltpu.VMEM((rows, depth), jnp.bfloat16),
            pltpu.VMEM((rows * HEAD_ROWS, HD), jnp.float32),
        ],
        compiler_params=pltpu.CompilerParams(vmem_limit_bytes=12 * MIB),
        cost_estimate=pl.CostEstimate(
            flops=2 * rows * up.size, bytes_accessed=2 * up.size, transcendentals=0
        ),
    )(*parts, *evens, number, up)
    return outs[:host_count], outs[host_count:]


def finish_kernel(base_count, back_count, place_ref, residual_ref, *refs):
    bases, backs = refs[:base_count], refs[base_count : base_count + back_count]
    more, refs = refs[base_count + back_count : -5], refs[-5:]
    out_hbm, tiles, sorted_tiles, out_ref, sem = refs
    row_count, columns = residual_ref.shape
    size = backs[0].shape[0]
    for k in range(back_count):
        tiles[k * size : (k + 1) * size] = backs[k][...].astype(jnp.float32)
    tiles[back_count * size :] = jnp.zeros((HEAD_ROWS, HD), jnp.float32)
    for r in range(row_count):
        where = pl.multiple_of(place_ref[r] * HEAD_ROWS, HEAD_ROWS)
        sorted_tiles[r * HEAD_ROWS : (r + 1) * HEAD_ROWS] = tiles[pl.ds(where, HEAD_ROWS), :]
    moves = []
    for j in range(columns // HD):
        cut = slice(j * HD, (j + 1) * HD)
        total = sorted_tiles[pl.ds(j, row_count, stride=HEAD_ROWS), :]
        for m in more:
            total = total + m[:, cut]
        total = residual_ref[:, cut].astype(jnp.float32) + ADAPTER_SCALE * total
        for b in bases:
            total = total + b[:, cut].astype(jnp.float32)
        out_ref[:, cut] = total.astype(jnp.bfloat16)
        if j % 2 == 1:
            part = pl.ds((j - 1) * HD, 2 * HD)
            moves.append(
                pltpu.make_async_copy(out_ref.at[:, part], out_hbm.at[:, part], sem.at[j // 2])
            )
            moves[-1].start()
    for move in moves:
        move.wait()


def finish(place, residual, bases, backs, *more):
    spec = pl.BlockSpec(memory_space=pltpu.VMEM)
    size = backs[0].shape[0]
    return pl.pallas_call(
        functools.partial(finish_kernel, len(bases), len(backs)),
        name="finish",
        out_shape=pltpu.HBM(residual.shape, jnp.bfloat16),
        in_specs=[pl.BlockSpec(memory_space=pltpu.SMEM)]
        + [spec] * (1 + len(bases) + len(backs) + len(more)),
        out_specs=pl.BlockSpec(memory_space=pl.ANY),
        scratch_shapes=[
            pltpu.VMEM((len(backs) * size + HEAD_ROWS, HD), jnp.float32),
            pltpu.VMEM((residual.shape[0] * HEAD_ROWS, HD), jnp.float32),
            pltpu.VMEM(residual.shape, jnp.bfloat16),
            pltpu.SemaphoreType.DMA((residual.shape[1] // HD // 2,)),
        ],
        compiler_params=pltpu.CompilerParams(vmem_limit_bytes=8 * MIB),
    )(place, residual, *bases, *backs, *more)


def swap(value, axis, k):
    size = lax.axis_size(axis)
    return lax.ppermute(value, axis, [(i, i ^ k) for i in range(size)])


def swap_all(values, axis, ks):
    return [v if k == 0 else swap(v, axis, k) for v, k in zip(values, ks)]


def second_pass(attended, down, up, stock, slots, room, rest):
    owned_total, rank, feature_here = down.shape
    host_count = lax.axis_size("hst")
    tp_count = lax.axis_size("tp")
    row_count = attended.shape[0]
    adapter = stock[slots]
    owner = adapter // owned_total
    order = jnp.arange(row_count)
    same = (owner[:, None] == owner[None, :]) & (order[None, :] < order[:, None])
    before = jnp.sum(same, axis=1)
    target = jnp.where(before >= room, owner * rest + before - room, -1)
    place = (target[:, None] == jnp.arange(host_count * rest)[None, :]).astype(jnp.float32)
    number = (adapter % owned_total + 1).astype(jnp.float32)
    numbers = jnp.broadcast_to((place.T @ number)[:, None], (host_count * rest, LANES))
    rows = jnp.dot(
        place.T.astype(jnp.bfloat16), attended, preferred_element_type=jnp.float32
    ).astype(jnp.bfloat16)
    rows = jnp.concatenate([rows, numbers.astype(jnp.bfloat16)], axis=1)
    rows = lax.all_to_all(rows, "hst", split_axis=0, concat_axis=0, tiled=True)
    number = rows[:, feature_here].astype(jnp.int32)
    rows = rows[:, :feature_here]
    uses = number[:, None] == jnp.arange(1, owned_total + 1)[None, :]
    product = jnp.einsum("rd,akd->rak", rows, down, preferred_element_type=jnp.float32)
    partial_sum = jnp.sum(jnp.where(uses[:, :, None], product, 0), axis=1)
    shrunk = sum([partial_sum] + [swap(partial_sum, "tp", k) for k in range(1, tp_count)])
    spread = jnp.where(uses[:, :, None], shrunk.astype(jnp.bfloat16)[:, None, :], 0)
    raised = jnp.einsum("rak,aki->ri", spread, up, preferred_element_type=jnp.float32)
    back = lax.all_to_all(
        raised.astype(jnp.bfloat16), "hst", split_axis=0, concat_axis=0, tiled=True
    )
    return jnp.dot(place.astype(jnp.bfloat16), back, preferred_element_type=jnp.float32)


def local(
    queries,
    key_page_cache,
    value_page_cache,
    request_pages,
    context_length,
    output_weight,
    adapter_down_weight,
    adapter_up_weight,
    residual,
    host_slot_adapter,
    request_slot,
):
    owned_total, rank, feature_here = adapter_down_weight.shape
    host_count = lax.axis_size("hst")
    tp_count = lax.axis_size("tp")
    slot_total = host_slot_adapter.shape[0]
    most = pair_rows(slot_total, host_count)
    room = min(FIRST, most)
    (attended, place, down), blocks = attend(
        queries,
        key_page_cache,
        value_page_cache,
        request_pages.T,
        context_length,
        request_slot.reshape(1, -1),
        host_slot_adapter.reshape(1, slot_total),
        adapter_down_weight.reshape(owned_total * rank, feature_here),
        owned_total,
        host_count,
        room,
    )
    row_count = attended.shape[0]
    ks = partners(host_count)
    blocks = swap_all(blocks, "hst", ks)
    evens = tp_count // 2
    one = jax.ShapeDtypeStruct((row_count, feature_here), jnp.bfloat16)
    odd = jax.ShapeDtypeStruct((evens * row_count, feature_here), jnp.bfloat16)
    odd = base_half(odd_kernel, "base_odd", attended, output_weight, odd)
    blocks, odd = lax.optimization_barrier((blocks, odd))
    partial_sum, joint, number, over, up = shrink(
        blocks, down, odd, adapter_up_weight.reshape(owned_total * rank, -1), room
    )
    parts = [partial_sum, joint] + [partial_sum] * (tp_count - 2)
    parts = swap_all(parts, "tp", range(tp_count))
    even = base_half(even_kernel, "base_even", attended, output_weight, [one] * evens)
    parts, even = lax.optimization_barrier((parts, even))
    raised, bases = expand(parts, even, number, up, host_count)
    bases = swap_all(bases, "tp", range(0, tp_count, 2))
    late = host_count // 2 + 1
    last, bases = lax.optimization_barrier((raised[late:], bases))
    backs = swap_all([*raised[:late], *last], "hst", ks)
    if room == most:
        return finish(place, residual, bases, backs)

    def with_second(bases, backs):
        more = second_pass(
            attended,
            adapter_down_weight,
            adapter_up_weight,
            host_slot_adapter,
            request_slot[:, 0],
            room,
            up_to(most - room, 16),
        )
        return finish(place, residual, bases, backs, more)

    def first_only(bases, backs):
        return finish(place, residual, bases, backs)

    return lax.cond(over[0] > 0, with_second, first_only, bases, backs)


def solution(mesh):
    in_specs = (
        P("hst", "tp"),
        P("hst", None, "tp"),
        P("hst", None, "tp"),
        P("hst", None),
        P("hst"),
        P("tp", None),
        P("hst", None, "tp"),
        P("hst", None, "tp"),
        P("hst", "tp"),
        P("hst"),
        P("hst", None),
    )
    out_specs = P("hst", "tp")
    return jax.shard_map(local, mesh=mesh, in_specs=in_specs, out_specs=out_specs, check_vma=False)
```

```python
import functools
import math

import jax
import jax.numpy as jnp
from jax import lax
from jax.experimental import pallas as pl
from jax.experimental.pallas import tpu as pltpu
from jax.sharding import PartitionSpec as P

HD = 128
LANES = 128
HEAD_ROWS = 8
GROUP = 16
ADAPTER_SCALE = 2.0
CAP = 4
FIRST = 20
CHUNKS = 4

MIB = 1 << 20
NT = (((1,), (1,)), ((), ()))
TN = (((0,), (0,)), ((), ()))
NN = (((1,), (0,)), ((), ()))


def iota(shape, axis):
    return lax.broadcasted_iota(jnp.int32, shape, axis)


def pair_rows(slot_total, host_count):
    return CAP * (2 * slot_total // host_count)


def up_to(value, step):
    return -(-value // step) * step


def block_of(k, count):
    return jnp.where(k == 0, 0, count - k)


def partners(count):
    return [0, *range(count - 1, 0, -1)]


def copies(source, target, sem, count):
    cut = source.shape[0] // count
    return [
        pltpu.make_async_copy(
            source.at[pl.ds(i * cut, cut)], target.at[pl.ds(i * cut, cut)], sem.at[i]
        )
        for i in range(count)
    ]


def in_hbm(*arrays):
    return [pltpu.with_memory_space_constraint(a, pltpu.HBM) for a in arrays]


def attention_kernel(owned_total, host_count, room, *refs):
    pages_hbm, length_hbm, query_hbm, slot_hbm, stock_hbm, keys_hbm, values_hbm = refs[:7]
    down_hbm, up_hbm, attended_ref, place_ref, down_ref, up_ref = refs[7:13]
    block_refs, refs = refs[13 : 13 + host_count], refs[13 + host_count :]
    (
        pages_ref,
        length_ref,
        query_ref,
        slot_ref,
        stock_ref,
        keys,
        values,
        query_rows,
        outcome,
        packed,
        numbers,
        counts,
        spot_ref,
        places,
        small_sem,
        key_sem,
        value_sem,
        weight_sem,
    ) = refs
    row_count, feature_here = query_ref.shape
    page_total, page, kv_width = keys_hbm.shape
    heads = feature_here // HD
    kv_here = kv_width // HD
    share = heads // kv_here
    most_pages = pages_ref.shape[0]
    context = most_pages * page

    small_moves = [
        pltpu.make_async_copy(source, target, small_sem.at[i])
        for i, (source, target) in enumerate(
            (
                (query_hbm, query_ref),
                (slot_hbm, slot_ref),
                (stock_hbm, stock_ref),
                (pages_hbm, pages_ref),
                (length_hbm, length_ref),
            )
        )
    ]
    key_moves = copies(keys_hbm, keys, key_sem, CHUNKS)
    value_moves = copies(values_hbm, values, value_sem, CHUNKS)
    weight_moves = copies(down_hbm, down_ref, weight_sem.at[0], CHUNKS)
    weight_moves += copies(up_hbm, up_ref, weight_sem.at[1], CHUNKS)
    for move in small_moves + key_moves + value_moves:
        move.start()
    packed[...] = jnp.zeros_like(packed)
    numbers[...] = jnp.zeros_like(numbers)
    for o in range(host_count):
        counts[o] = 0
    for move in small_moves:
        move.wait()

    if heads < HEAD_ROWS:
        query_rows[...] = jnp.zeros_like(query_rows)
    for j in range(heads):
        query_rows[pl.ds(j, row_count, stride=HEAD_ROWS), :] = query_ref[
            :, j * HD : (j + 1) * HD
        ].astype(jnp.float32)

    me = lax.axis_index("hst")
    pad = up_to(room, 8)

    def count(r, most):
        adapter = stock_ref[0, slot_ref[0, r]]
        owner = lax.div(adapter, owned_total)
        before = counts[owner]
        counts[owner] = before + 1
        block = block_of(owner ^ me, host_count)
        fits = before < room
        spot = jnp.where(fits, block * room + before, host_count * room)
        spot_ref[r] = spot
        places[pl.ds(r, 1), :] = jnp.where(iota((1, places.shape[1]), 1) == spot, 1.0, 0.0)
        where = jnp.where(fits, block * pad + before, host_count * pad)
        number = jnp.full((1, LANES), adapter - owner * owned_total + 1, jnp.int32)
        numbers[pl.ds(where, 1), :] = number.astype(jnp.float32)
        return jnp.maximum(most, before)

    most = lax.fori_loop(0, row_count, count, jnp.int32(0))
    place_ref[...] = places[...].astype(jnp.bfloat16)
    over = jnp.where(jnp.full((8, LANES), most, jnp.int32) >= room, 1.0, 0.0)

    for move in key_moves:
        move.wait()
    for move in weight_moves:
        move.start()

    head_of = iota((HEAD_ROWS, HD), 0) // share

    def tile_of(r):
        return pl.ds(pl.multiple_of(r * HEAD_ROWS, HEAD_ROWS), HEAD_ROWS)

    def some_scores(step, carry):
        first = step * GROUP
        scores = []
        for i in range(GROUP):
            r = first + i
            rows = query_rows[tile_of(r), :]
            wide = jnp.concatenate(
                [jnp.where(head_of == c, rows, 0.0) for c in range(kv_here)], axis=1
            ).astype(jnp.bfloat16)
            held = jnp.concatenate([keys[pages_ref[p, r]] for p in range(most_pages)], axis=0)
            part = lax.dot_general(wide, held, NT, preferred_element_type=jnp.float32)
            live = iota((HEAD_ROWS, context), 1) < length_ref[r]
            scores.append(jnp.where(live, part * (1.0 / math.sqrt(HD)), -jnp.inf))
        score = jnp.concatenate(scores, axis=0)
        weight = jnp.exp(score - jnp.max(score, axis=1, keepdims=True))
        weight = weight / jnp.sum(weight, axis=1, keepdims=True)
        size = GROUP * HEAD_ROWS
        outcome[pl.ds(pl.multiple_of(step * size, size), size), :] = weight
        return carry

    def some_values(step, carry):
        first = step * GROUP
        for i in range(GROUP):
            r = first + i
            held = jnp.concatenate([values[pages_ref[p, r]] for p in range(most_pages)], axis=0)
            part = lax.dot_general(
                outcome[tile_of(r), :].astype(jnp.bfloat16),
                held,
                NN,
                preferred_element_type=jnp.float32,
            )
            result = part[:, :HD]
            for c in range(1, kv_here):
                result = jnp.where(head_of == c, part[:, c * HD : (c + 1) * HD], result)
            outcome[tile_of(r), :] = result
            packed[tile_of(spot_ref[r]), :] = result
        return carry

    lax.fori_loop(0, row_count // GROUP, some_scores, 0)
    for move in value_moves:
        move.wait()
    lax.fori_loop(0, row_count // GROUP, some_values, 0)

    lane = iota((8, LANES), 1)
    size = room * HEAD_ROWS
    for k in range(host_count):
        tile = jnp.where(lane == LANES - 1, over, 0.0)
        for b in range(pad // 8):
            tile = jnp.where(lane == b, numbers[k * pad + 8 * b : k * pad + 8 * b + 8], tile)
        block_refs[k][...] = jnp.concatenate(
            [packed[k * size : (k + 1) * size], tile], axis=0
        ).astype(jnp.bfloat16)
    for j in range(heads):
        attended_ref[:, j * HD : (j + 1) * HD] = outcome[
            pl.ds(j, row_count, stride=HEAD_ROWS), :
        ].astype(jnp.bfloat16)
    for move in weight_moves:
        move.wait()


def attend(
    queries, keys, values, pages, lengths, slots, stock, down, up, owned_total, hosts, room
):
    row_count, feature_here = queries.shape
    spec = pl.BlockSpec(memory_space=pltpu.VMEM)
    far = pl.BlockSpec(memory_space=pl.ANY)
    block = jax.ShapeDtypeStruct((room * HEAD_ROWS + 8, LANES), jnp.bfloat16)
    outs = pl.pallas_call(
        functools.partial(attention_kernel, owned_total, hosts, room),
        name="attend",
        out_shape=[
            jax.ShapeDtypeStruct((row_count, feature_here), jnp.bfloat16),
            jax.ShapeDtypeStruct((row_count, up_to(hosts * room, LANES)), jnp.bfloat16),
            pltpu.VMEM(down.shape, jnp.bfloat16),
            pltpu.VMEM(up.shape, jnp.bfloat16),
        ]
        + [block] * hosts,
        in_specs=[far] * 9,
        out_specs=[spec] * (4 + hosts),
        scratch_shapes=[
            pltpu.SMEM(pages.shape, jnp.int32),
            pltpu.SMEM(lengths.shape, jnp.int32),
            pltpu.VMEM(queries.shape, jnp.bfloat16),
            pltpu.SMEM(slots.shape, jnp.int32),
            pltpu.SMEM(stock.shape, jnp.int32),
            pltpu.VMEM(keys.shape, jnp.bfloat16),
            pltpu.VMEM(values.shape, jnp.bfloat16),
            pltpu.VMEM((row_count * HEAD_ROWS, HD), jnp.float32),
            pltpu.VMEM((row_count * HEAD_ROWS, HD), jnp.float32),
            pltpu.VMEM(((hosts * room + 1) * HEAD_ROWS, HD), jnp.float32),
            pltpu.VMEM((hosts * up_to(room, 8) + 8, LANES), jnp.float32),
            pltpu.SMEM((hosts,), jnp.int32),
            pltpu.SMEM((row_count,), jnp.int32),
            pltpu.VMEM((row_count, up_to(hosts * room, LANES)), jnp.float32),
            pltpu.SemaphoreType.DMA((5,)),
            pltpu.SemaphoreType.DMA((CHUNKS,)),
            pltpu.SemaphoreType.DMA((CHUNKS,)),
            pltpu.SemaphoreType.DMA((2, CHUNKS)),
        ],
        compiler_params=pltpu.CompilerParams(vmem_limit_bytes=24 * MIB),
        cost_estimate=pl.CostEstimate(
            flops=4 * row_count * HEAD_ROWS * 128 * feature_here,
            bytes_accessed=4 * keys.size + 4 * down.size,
            transcendentals=row_count * HEAD_ROWS * 128,
        ),
    )(*in_hbm(pages, lengths, queries, slots, stock, keys, values, down, up))
    return outs[:4], outs[4:]


def base_moves(weight_hbm, weight, sem, parity):
    count, parts = sem.shape
    me = lax.axis_index("tp")
    depth, width = weight.shape[1:]
    cut = depth // parts
    moves = []
    for i in range(count):
        columns = pl.ds(pl.multiple_of((me ^ (2 * i + parity)) * width, width), width)
        for part in range(parts):
            rows = pl.ds(part * cut, cut)
            moves.append(
                pltpu.make_async_copy(
                    weight_hbm.at[rows, columns], weight.at[i, rows], sem.at[i, part]
                )
            )
    return moves


def odd_kernel(attended_ref, weight_hbm, out_ref, weight, sem):
    moves = base_moves(weight_hbm, weight, sem, 1)
    for move in moves:
        move.start()
    count, parts = sem.shape
    rows = attended_ref[...]
    for i in range(count):
        for move in moves[i * parts : (i + 1) * parts]:
            move.wait()
        out_ref[i * rows.shape[0] : (i + 1) * rows.shape[0]] = jnp.dot(
            rows, weight[i], preferred_element_type=jnp.float32
        ).astype(jnp.bfloat16)


def even_kernel(attended_ref, weight_hbm, *refs):
    outs, (weight, sem) = refs[:-2], refs[-2:]
    moves = base_moves(weight_hbm, weight, sem, 0)
    for move in moves:
        move.start()
    count, parts = sem.shape
    rows = attended_ref[...]
    for i in range(count):
        for move in moves[i * parts : (i + 1) * parts]:
            move.wait()
        outs[i][...] = jnp.dot(rows, weight[i], preferred_element_type=jnp.float32).astype(
            jnp.bfloat16
        )


def base_half(kernel, name, attended, weight, out_shape):
    row_count, depth = attended.shape
    count = weight.shape[1] // depth // 2
    spec = pl.BlockSpec(memory_space=pltpu.VMEM)
    return pl.pallas_call(
        kernel,
        name=name,
        out_shape=out_shape,
        in_specs=[spec, pl.BlockSpec(memory_space=pl.ANY)],
        out_specs=jax.tree.map(lambda _: spec, out_shape),
        scratch_shapes=[
            pltpu.VMEM((count, depth, depth), jnp.bfloat16),
            pltpu.SemaphoreType.DMA((count, 8)),
        ],
        compiler_params=pltpu.CompilerParams(vmem_limit_bytes=12 * MIB),
        cost_estimate=pl.CostEstimate(
            flops=row_count * weight.size, bytes_accessed=weight.size, transcendentals=0
        ),
    )(attended, *in_hbm(weight))


def shrink_kernel(host_count, room, *refs):
    blocks = refs[:host_count]
    down_ref, odd_ref, partial_ref, joint_ref, number_ref, over_ref = refs[host_count:-2]
    tiles, total = refs[-2:]
    heads = down_ref.shape[1] // HD
    rows_all = host_count * room
    size = room * HEAD_ROWS
    width = 256
    rank = LANES // 2
    lane = iota((8, LANES), 1)
    over = jnp.zeros((8, LANES), jnp.float32)
    for k in range(host_count):
        tiles[k * size : (k + 1) * size] = blocks[k][:size].astype(jnp.float32)
        tile = blocks[k][size:].astype(jnp.float32)
        over = jnp.maximum(over, jnp.where(lane == LANES - 1, tile, 0.0))
        for b in range(up_to(room, 8) // 8):
            rest = min(8, room - 8 * b)
            column = jnp.sum(jnp.where(lane == b, tile, 0.0), axis=1, keepdims=True)
            column = jnp.broadcast_to(column, (8, LANES))
            number_ref[k * room + 8 * b : k * room + 8 * b + rest] = column[:rest]
    over_ref[...] = over
    rows = jnp.concatenate(
        [tiles[pl.ds(j, rows_all, stride=HEAD_ROWS), :].astype(jnp.bfloat16) for j in range(heads)],
        axis=1,
    )
    number = number_ref[...]
    own = (iota(number.shape, 1) // rank).astype(jnp.float32) + 1.0
    for step in range(down_ref.shape[0] // width):
        product = lax.dot_general(
            rows,
            down_ref[step * width : (step + 1) * width],
            NT,
            preferred_element_type=jnp.float32,
        )
        add = jnp.zeros_like(number) if step == 0 else total[...]
        for i in range(width // LANES):
            piece = product[:, i * LANES : (i + 1) * LANES]
            first = 2.0 * (step * (width // LANES) + i)
            add = jnp.where(number == own + first, piece + add, add)
        total[...] = add
    full = total[...]
    full = full + pltpu.roll(full, rank, 1)
    half = rows_all // 2
    left = iota((half, LANES), 1) < rank
    partial_ref[...] = jnp.where(left, full[:half], full[half:]).astype(jnp.bfloat16)
    joint_ref[:half] = partial_ref[...]
    odd_rows = odd_ref.shape[0]
    for j in range(odd_ref.shape[1] // LANES):
        first = half + j * odd_rows
        joint_ref[first : first + odd_rows] = odd_ref[:, j * LANES : (j + 1) * LANES]


def shrink(blocks, down, odd, room):
    host_count = len(blocks)
    rows = host_count * room
    spec = pl.BlockSpec(memory_space=pltpu.VMEM)
    return pl.pallas_call(
        functools.partial(shrink_kernel, host_count, room),
        name="shrink",
        out_shape=(
            jax.ShapeDtypeStruct((rows // 2, LANES), jnp.bfloat16),
            jax.ShapeDtypeStruct((rows // 2 + odd.size // LANES, LANES), jnp.bfloat16),
            jax.ShapeDtypeStruct((rows, LANES), jnp.float32),
            jax.ShapeDtypeStruct((8, LANES), jnp.float32),
        ),
        in_specs=[spec] * (host_count + 2),
        out_specs=(spec,) * 4,
        scratch_shapes=[
            pltpu.VMEM((rows * HEAD_ROWS, HD), jnp.float32),
            pltpu.VMEM((rows, LANES), jnp.float32),
        ],
        compiler_params=pltpu.CompilerParams(vmem_limit_bytes=12 * MIB),
        cost_estimate=pl.CostEstimate(
            flops=2 * rows * down.size, bytes_accessed=2 * down.size, transcendentals=0
        ),
    )(*blocks, down, odd)


def expand_kernel(part_count, even_count, host_count, *refs):
    parts, refs = refs[:part_count], refs[part_count:]
    evens, (number_ref, up_ref), refs = refs[:even_count], refs[even_count:][:2], refs[even_count + 2 :]
    outs, sums, (spread, tiles) = refs[:host_count], refs[host_count:-2], refs[-2:]
    rows, columns = number_ref.shape[0], up_ref.shape[1]
    width = min(256, columns)
    rank = LANES // 2
    half = rows // 2
    full = parts[0][...].astype(jnp.float32)
    for p in parts[1:]:
        full = full + p[:half].astype(jnp.float32)
    other = pltpu.roll(full, rank, 1)
    left = iota(full.shape, 1) < rank
    both = jnp.concatenate(
        [jnp.where(left, full, other), jnp.where(left, other, full)], axis=0
    )
    number = number_ref[...]
    own = (iota(number.shape, 1) // rank).astype(jnp.float32) + 1.0
    for i in range(spread.shape[1] // LANES):
        spread[:, i * LANES : (i + 1) * LANES] = jnp.where(
            number == own + 2.0 * i, both, 0.0
        ).astype(jnp.bfloat16)
    if columns // HD < HEAD_ROWS:
        tiles[...] = jnp.zeros_like(tiles)
    for i in range(columns // width):
        result = jnp.dot(
            spread[...],
            up_ref[:, i * width : (i + 1) * width],
            preferred_element_type=jnp.float32,
        )
        for j in range(width // HD):
            tiles[pl.ds(i * (width // HD) + j, rows, stride=HEAD_ROWS), :] = result[
                :, j * HD : (j + 1) * HD
            ]
    size = rows // host_count * HEAD_ROWS
    for k in range(host_count):
        outs[k][...] = tiles[k * size : (k + 1) * size].astype(jnp.bfloat16)
    row_count = evens[0].shape[0]
    for i in range(even_count):
        for j in range(columns // LANES):
            first = half + (j * even_count + i) * row_count
            cut = slice(j * LANES, (j + 1) * LANES)
            sums[i][:, cut] = (
                evens[i][:, cut].astype(jnp.float32)
                + parts[1][first : first + row_count].astype(jnp.float32)
            ).astype(jnp.bfloat16)


def expand(parts, evens, number, up, host_count):
    rows = number.shape[0]
    depth, columns = up.shape
    spec = pl.BlockSpec(memory_space=pltpu.VMEM)
    block = jax.ShapeDtypeStruct((rows // host_count * HEAD_ROWS, HD), jnp.bfloat16)
    outs = pl.pallas_call(
        functools.partial(expand_kernel, len(parts), len(evens), host_count),
        name="expand",
        out_shape=[block] * host_count
        + [jax.ShapeDtypeStruct(e.shape, jnp.bfloat16) for e in evens],
        in_specs=[spec] * (len(parts) + len(evens) + 2),
        out_specs=[spec] * (host_count + len(evens)),
        scratch_shapes=[
            pltpu.VMEM((rows, depth), jnp.bfloat16),
            pltpu.VMEM((rows * HEAD_ROWS, HD), jnp.float32),
        ],
        compiler_params=pltpu.CompilerParams(vmem_limit_bytes=12 * MIB),
        cost_estimate=pl.CostEstimate(
            flops=2 * rows * up.size, bytes_accessed=2 * up.size, transcendentals=0
        ),
    )(*parts, *evens, number, up)
    return outs[:host_count], outs[host_count:]


def finish_kernel(base_count, back_count, place_ref, residual_ref, *refs):
    bases, backs = refs[:base_count], refs[base_count : base_count + back_count]
    more, (out_ref, tiles) = refs[base_count + back_count : -2], refs[-2:]
    columns = residual_ref.shape[1]
    size = backs[0].shape[0]
    for k in range(back_count):
        tiles[k * size : (k + 1) * size] = backs[k][...].astype(jnp.float32)
    used = back_count * size
    if used < tiles.shape[0]:
        tiles[used:] = jnp.zeros((tiles.shape[0] - used, HD), jnp.float32)
    place = place_ref[...]
    for j in range(columns // HD):
        cut = slice(j * HD, (j + 1) * HD)
        column = tiles[pl.ds(j, place.shape[1], stride=HEAD_ROWS), :].astype(jnp.bfloat16)
        total = jnp.dot(place, column, preferred_element_type=jnp.float32)
        for m in more:
            total = total + m[:, cut]
        total = residual_ref[:, cut].astype(jnp.float32) + ADAPTER_SCALE * total
        for b in bases:
            total = total + b[:, cut].astype(jnp.float32)
        out_ref[:, cut] = total.astype(jnp.bfloat16)


def finish(place, residual, bases, backs, *more):
    spec = pl.BlockSpec(memory_space=pltpu.VMEM)
    return pl.pallas_call(
        functools.partial(finish_kernel, len(bases), len(backs)),
        name="finish",
        out_shape=pltpu.HBM(residual.shape, jnp.bfloat16),
        in_specs=[spec] * (2 + len(bases) + len(backs) + len(more)),
        out_specs=spec,
        scratch_shapes=[
            pltpu.VMEM((place.shape[1] * HEAD_ROWS, HD), jnp.float32),
        ],
        compiler_params=pltpu.CompilerParams(vmem_limit_bytes=8 * MIB),
    )(place, residual, *bases, *backs, *more)


def swap(value, axis, k):
    size = lax.axis_size(axis)
    return lax.ppermute(value, axis, [(i, i ^ k) for i in range(size)])


def swap_all(values, axis, ks):
    return [v if k == 0 else swap(v, axis, k) for v, k in zip(values, ks)]


def second_pass(attended, down, up, stock, slots, room, rest):
    owned_total, rank, feature_here = down.shape
    host_count = lax.axis_size("hst")
    tp_count = lax.axis_size("tp")
    row_count = attended.shape[0]
    adapter = stock[slots]
    owner = adapter // owned_total
    order = jnp.arange(row_count)
    same = (owner[:, None] == owner[None, :]) & (order[None, :] < order[:, None])
    before = jnp.sum(same, axis=1)
    target = jnp.where(before >= room, owner * rest + before - room, -1)
    place = (target[:, None] == jnp.arange(host_count * rest)[None, :]).astype(jnp.float32)
    number = (adapter % owned_total + 1).astype(jnp.float32)
    numbers = jnp.broadcast_to((place.T @ number)[:, None], (host_count * rest, LANES))
    rows = jnp.dot(
        place.T.astype(jnp.bfloat16), attended, preferred_element_type=jnp.float32
    ).astype(jnp.bfloat16)
    rows = jnp.concatenate([rows, numbers.astype(jnp.bfloat16)], axis=1)
    rows = lax.all_to_all(rows, "hst", split_axis=0, concat_axis=0, tiled=True)
    number = rows[:, feature_here].astype(jnp.int32)
    rows = rows[:, :feature_here]
    uses = number[:, None] == jnp.arange(1, owned_total + 1)[None, :]
    product = jnp.einsum("rd,akd->rak", rows, down, preferred_element_type=jnp.float32)
    partial_sum = jnp.sum(jnp.where(uses[:, :, None], product, 0), axis=1)
    shrunk = sum([partial_sum] + [swap(partial_sum, "tp", k) for k in range(1, tp_count)])
    spread = jnp.where(uses[:, :, None], shrunk.astype(jnp.bfloat16)[:, None, :], 0)
    raised = jnp.einsum("rak,aki->ri", spread, up, preferred_element_type=jnp.float32)
    back = lax.all_to_all(
        raised.astype(jnp.bfloat16), "hst", split_axis=0, concat_axis=0, tiled=True
    )
    return jnp.dot(place.astype(jnp.bfloat16), back, preferred_element_type=jnp.float32)


def local(
    queries,
    key_page_cache,
    value_page_cache,
    request_pages,
    context_length,
    output_weight,
    adapter_down_weight,
    adapter_up_weight,
    residual,
    host_slot_adapter,
    request_slot,
):
    owned_total, rank, feature_here = adapter_down_weight.shape
    host_count = lax.axis_size("hst")
    tp_count = lax.axis_size("tp")
    slot_total = host_slot_adapter.shape[0]
    most = pair_rows(slot_total, host_count)
    room = min(FIRST, most)
    (attended, place, down, up), blocks = attend(
        queries,
        key_page_cache,
        value_page_cache,
        request_pages.T,
        context_length,
        request_slot.reshape(1, -1),
        host_slot_adapter.reshape(1, slot_total),
        adapter_down_weight.reshape(owned_total * rank, feature_here),
        adapter_up_weight.reshape(owned_total * rank, -1),
        owned_total,
        host_count,
        room,
    )
    row_count = attended.shape[0]
    ks = partners(host_count)
    blocks = swap_all(blocks, "hst", ks)
    evens = tp_count // 2
    one = jax.ShapeDtypeStruct((row_count, feature_here), jnp.bfloat16)
    odd = jax.ShapeDtypeStruct((evens * row_count, feature_here), jnp.bfloat16)
    odd = base_half(odd_kernel, "base_odd", attended, output_weight, odd)
    blocks, odd = lax.optimization_barrier((blocks, odd))
    partial_sum, joint, number, over = shrink(blocks, down, odd, room)
    parts = [partial_sum, joint] + [partial_sum] * (tp_count - 2)
    parts = swap_all(parts, "tp", range(tp_count))
    even = base_half(even_kernel, "base_even", attended, output_weight, [one] * evens)
    parts, even = lax.optimization_barrier((parts, even))
    raised, bases = expand(parts, even, number, up, host_count)
    bases = swap_all(bases, "tp", range(0, tp_count, 2))
    late = host_count // 2 + 1
    last, bases = lax.optimization_barrier((raised[late:], bases))
    backs = swap_all([*raised[:late], *last], "hst", ks)
    if room == most:
        return finish(place, residual, bases, backs)

    def with_second(bases, backs):
        more = second_pass(
            attended,
            adapter_down_weight,
            adapter_up_weight,
            host_slot_adapter,
            request_slot[:, 0],
            room,
            up_to(most - room, 16),
        )
        return finish(place, residual, bases, backs, more)

    def first_only(bases, backs):
        return finish(place, residual, bases, backs)

    return lax.cond(jnp.max(over) > 0, with_second, first_only, bases, backs)


def solution(mesh):
    in_specs = (
        P("hst", "tp"),
        P("hst", None, "tp"),
        P("hst", None, "tp"),
        P("hst", None),
        P("hst"),
        P("tp", None),
        P("hst", None, "tp"),
        P("hst", None, "tp"),
        P("hst", "tp"),
        P("hst"),
        P("hst", None),
    )
    out_specs = P("hst", "tp")
    return jax.shard_map(local, mesh=mesh, in_specs=in_specs, out_specs=out_specs, check_vma=False)
```

```python
import functools
import math

import jax
import jax.numpy as jnp
from jax import lax
from jax.experimental import pallas as pl
from jax.experimental.pallas import tpu as pltpu
from jax.sharding import PartitionSpec as P

HD = 128
LANES = 128
HEAD_ROWS = 8
GROUP = 16
ADAPTER_SCALE = 2.0
CAP = 4
FIRST = 20
CHUNKS = 4

MIB = 1 << 20
NT = (((1,), (1,)), ((), ()))
TN = (((0,), (0,)), ((), ()))
NN = (((1,), (0,)), ((), ()))


def iota(shape, axis):
    return lax.broadcasted_iota(jnp.int32, shape, axis)


def pair_rows(slot_total, host_count):
    return CAP * (2 * slot_total // host_count)


def up_to(value, step):
    return -(-value // step) * step


def block_of(k, count):
    return jnp.where(k == 0, 0, count - k)


def partners(count):
    return [0, *range(count - 1, 0, -1)]


def copies(source, target, sem, count):
    cut = source.shape[0] // count
    return [
        pltpu.make_async_copy(
            source.at[pl.ds(i * cut, cut)], target.at[pl.ds(i * cut, cut)], sem.at[i]
        )
        for i in range(count)
    ]


def in_hbm(*arrays):
    return [pltpu.with_memory_space_constraint(a, pltpu.HBM) for a in arrays]


def attention_kernel(owned_total, host_count, room, *refs):
    pages_hbm, length_hbm, query_hbm, slot_hbm, stock_hbm, keys_hbm, values_hbm = refs[:7]
    down_hbm, up_hbm, attended_ref, place_ref, down_ref, up_ref = refs[7:13]
    block_refs, refs = refs[13 : 13 + host_count], refs[13 + host_count :]
    (
        pages_ref,
        length_ref,
        query_ref,
        slot_ref,
        stock_ref,
        keys,
        values,
        query_rows,
        outcome,
        packed,
        numbers,
        counts,
        spot_ref,
        places,
        small_sem,
        key_sem,
        value_sem,
        weight_sem,
    ) = refs
    row_count, feature_here = query_ref.shape
    page_total, page, kv_width = keys_hbm.shape
    heads = feature_here // HD
    kv_here = kv_width // HD
    share = heads // kv_here
    most_pages = pages_ref.shape[0]
    context = most_pages * page

    small_moves = [
        pltpu.make_async_copy(source, target, small_sem.at[i])
        for i, (source, target) in enumerate(
            (
                (query_hbm, query_ref),
                (slot_hbm, slot_ref),
                (stock_hbm, stock_ref),
                (pages_hbm, pages_ref),
                (length_hbm, length_ref),
            )
        )
    ]
    key_moves = copies(keys_hbm, keys, key_sem, CHUNKS)
    value_moves = copies(values_hbm, values, value_sem, CHUNKS)
    weight_moves = copies(down_hbm, down_ref, weight_sem.at[0], CHUNKS)
    weight_moves += copies(up_hbm, up_ref, weight_sem.at[1], CHUNKS)
    for move in small_moves + key_moves + value_moves:
        move.start()
    packed[...] = jnp.zeros_like(packed)
    numbers[...] = jnp.zeros_like(numbers)
    for o in range(host_count):
        counts[o] = 0
    for move in small_moves:
        move.wait()

    if heads < HEAD_ROWS:
        query_rows[...] = jnp.zeros_like(query_rows)
    for j in range(heads):
        query_rows[pl.ds(j, row_count, stride=HEAD_ROWS), :] = query_ref[
            :, j * HD : (j + 1) * HD
        ].astype(jnp.float32)

    me = lax.axis_index("hst")
    pad = up_to(room, 8)

    def count(r, most):
        adapter = stock_ref[0, slot_ref[0, r]]
        if owned_total & (owned_total - 1) == 0:
            owner = lax.shift_right_logical(adapter, jnp.int32(owned_total.bit_length() - 1))
        else:
            owner = lax.div(adapter, owned_total)
        before = counts[owner]
        counts[owner] = before + 1
        block = block_of(owner ^ me, host_count)
        fits = before < room
        spot = jnp.where(fits, block * room + before, host_count * room)
        spot_ref[r] = spot
        places[pl.ds(r, 1), :] = jnp.where(iota((1, places.shape[1]), 1) == spot, 1.0, 0.0)
        where = jnp.where(fits, block * pad + before, host_count * pad)
        number = jnp.full((1, LANES), adapter - owner * owned_total + 1, jnp.int32)
        numbers[pl.ds(where, 1), :] = number.astype(jnp.float32)
        return jnp.maximum(most, before)

    most = lax.fori_loop(0, row_count, count, jnp.int32(0), unroll=8)
    place_ref[...] = places[...].astype(jnp.bfloat16)
    over = jnp.where(jnp.full((8, LANES), most, jnp.int32) >= room, 1.0, 0.0)

    for move in key_moves:
        move.wait()
    for move in weight_moves:
        move.start()

    head_of = iota((HEAD_ROWS, HD), 0) // share

    def tile_of(r):
        return pl.ds(pl.multiple_of(r * HEAD_ROWS, HEAD_ROWS), HEAD_ROWS)

    def some_scores(step, carry):
        first = step * GROUP
        scores = []
        for i in range(GROUP):
            r = first + i
            rows = query_rows[tile_of(r), :]
            wide = jnp.concatenate(
                [jnp.where(head_of == c, rows, 0.0) for c in range(kv_here)], axis=1
            ).astype(jnp.bfloat16)
            held = jnp.concatenate([keys[pages_ref[p, r]] for p in range(most_pages)], axis=0)
            part = lax.dot_general(wide, held, NT, preferred_element_type=jnp.float32)
            live = iota((HEAD_ROWS, context), 1) < length_ref[r]
            scores.append(jnp.where(live, part * (1.0 / math.sqrt(HD)), -jnp.inf))
        score = jnp.concatenate(scores, axis=0)
        weight = jnp.exp(score - jnp.max(score, axis=1, keepdims=True))
        weight = weight / jnp.sum(weight, axis=1, keepdims=True)
        size = GROUP * HEAD_ROWS
        outcome[pl.ds(pl.multiple_of(step * size, size), size), :] = weight
        return carry

    def some_values(step, carry):
        first = step * GROUP
        for i in range(GROUP):
            r = first + i
            held = jnp.concatenate([values[pages_ref[p, r]] for p in range(most_pages)], axis=0)
            part = lax.dot_general(
                outcome[tile_of(r), :].astype(jnp.bfloat16),
                held,
                NN,
                preferred_element_type=jnp.float32,
            )
            result = part[:, :HD]
            for c in range(1, kv_here):
                result = jnp.where(head_of == c, part[:, c * HD : (c + 1) * HD], result)
            outcome[tile_of(r), :] = result
            packed[tile_of(spot_ref[r]), :] = result
        return carry

    lax.fori_loop(0, row_count // GROUP, some_scores, 0)
    for move in value_moves:
        move.wait()
    lax.fori_loop(0, row_count // GROUP, some_values, 0)

    lane = iota((8, LANES), 1)
    size = room * HEAD_ROWS
    for k in range(host_count):
        tile = jnp.where(lane == LANES - 1, over, 0.0)
        for b in range(pad // 8):
            tile = jnp.where(lane == b, numbers[k * pad + 8 * b : k * pad + 8 * b + 8], tile)
        block_refs[k][...] = jnp.concatenate(
            [packed[k * size : (k + 1) * size], tile], axis=0
        ).astype(jnp.bfloat16)
    for j in range(heads):
        attended_ref[:, j * HD : (j + 1) * HD] = outcome[
            pl.ds(j, row_count, stride=HEAD_ROWS), :
        ].astype(jnp.bfloat16)
    for move in weight_moves:
        move.wait()


def attend(
    queries, keys, values, pages, lengths, slots, stock, down, up, owned_total, hosts, room
):
    row_count, feature_here = queries.shape
    spec = pl.BlockSpec(memory_space=pltpu.VMEM)
    far = pl.BlockSpec(memory_space=pl.ANY)
    block = jax.ShapeDtypeStruct((room * HEAD_ROWS + 8, LANES), jnp.bfloat16)
    outs = pl.pallas_call(
        functools.partial(attention_kernel, owned_total, hosts, room),
        name="attend",
        out_shape=[
            jax.ShapeDtypeStruct((row_count, feature_here), jnp.bfloat16),
            jax.ShapeDtypeStruct((row_count, up_to(hosts * room, LANES)), jnp.bfloat16),
            pltpu.VMEM(down.shape, jnp.bfloat16),
            pltpu.VMEM(up.shape, jnp.bfloat16),
        ]
        + [block] * hosts,
        in_specs=[far] * 9,
        out_specs=[spec] * (4 + hosts),
        scratch_shapes=[
            pltpu.SMEM(pages.shape, jnp.int32),
            pltpu.SMEM(lengths.shape, jnp.int32),
            pltpu.VMEM(queries.shape, jnp.bfloat16),
            pltpu.SMEM(slots.shape, jnp.int32),
            pltpu.SMEM(stock.shape, jnp.int32),
            pltpu.VMEM(keys.shape, jnp.bfloat16),
            pltpu.VMEM(values.shape, jnp.bfloat16),
            pltpu.VMEM((row_count * HEAD_ROWS, HD), jnp.float32),
            pltpu.VMEM((row_count * HEAD_ROWS, HD), jnp.float32),
            pltpu.VMEM(((hosts * room + 1) * HEAD_ROWS, HD), jnp.float32),
            pltpu.VMEM((hosts * up_to(room, 8) + 8, LANES), jnp.float32),
            pltpu.SMEM((hosts,), jnp.int32),
            pltpu.SMEM((row_count,), jnp.int32),
            pltpu.VMEM((row_count, up_to(hosts * room, LANES)), jnp.float32),
            pltpu.SemaphoreType.DMA((5,)),
            pltpu.SemaphoreType.DMA((CHUNKS,)),
            pltpu.SemaphoreType.DMA((CHUNKS,)),
            pltpu.SemaphoreType.DMA((2, CHUNKS)),
        ],
        compiler_params=pltpu.CompilerParams(vmem_limit_bytes=24 * MIB),
        cost_estimate=pl.CostEstimate(
            flops=4 * row_count * HEAD_ROWS * 128 * feature_here,
            bytes_accessed=4 * keys.size + 4 * down.size,
            transcendentals=row_count * HEAD_ROWS * 128,
        ),
    )(*in_hbm(pages, lengths, queries, slots, stock, keys, values, down, up))
    return outs[:4], outs[4:]


def base_moves(weight_hbm, weight, sem, parity):
    count, parts = sem.shape
    me = lax.axis_index("tp")
    depth, width = weight.shape[1:]
    cut = depth // parts
    moves = []
    for i in range(count):
        columns = pl.ds(pl.multiple_of((me ^ (2 * i + parity)) * width, width), width)
        for part in range(parts):
            rows = pl.ds(part * cut, cut)
            moves.append(
                pltpu.make_async_copy(
                    weight_hbm.at[rows, columns], weight.at[i, rows], sem.at[i, part]
                )
            )
    return moves


def odd_kernel(attended_ref, weight_hbm, out_ref, weight, sem):
    moves = base_moves(weight_hbm, weight, sem, 1)
    for move in moves:
        move.start()
    count, parts = sem.shape
    rows = attended_ref[...]
    for i in range(count):
        for move in moves[i * parts : (i + 1) * parts]:
            move.wait()
        out_ref[i * rows.shape[0] : (i + 1) * rows.shape[0]] = jnp.dot(
            rows, weight[i], preferred_element_type=jnp.float32
        ).astype(jnp.bfloat16)


def even_kernel(attended_ref, weight_hbm, *refs):
    outs, (weight, sem) = refs[:-2], refs[-2:]
    moves = base_moves(weight_hbm, weight, sem, 0)
    for move in moves:
        move.start()
    count, parts = sem.shape
    rows = attended_ref[...]
    for i in range(count):
        for move in moves[i * parts : (i + 1) * parts]:
            move.wait()
        outs[i][...] = jnp.dot(rows, weight[i], preferred_element_type=jnp.float32).astype(
            jnp.bfloat16
        )


def base_half(kernel, name, attended, weight, out_shape):
    row_count, depth = attended.shape
    count = weight.shape[1] // depth // 2
    spec = pl.BlockSpec(memory_space=pltpu.VMEM)
    return pl.pallas_call(
        kernel,
        name=name,
        out_shape=out_shape,
        in_specs=[spec, pl.BlockSpec(memory_space=pl.ANY)],
        out_specs=jax.tree.map(lambda _: spec, out_shape),
        scratch_shapes=[
            pltpu.VMEM((count, depth, depth), jnp.bfloat16),
            pltpu.SemaphoreType.DMA((count, 8)),
        ],
        compiler_params=pltpu.CompilerParams(vmem_limit_bytes=12 * MIB),
        cost_estimate=pl.CostEstimate(
            flops=row_count * weight.size, bytes_accessed=weight.size, transcendentals=0
        ),
    )(attended, *in_hbm(weight))


def shrink_kernel(host_count, room, *refs):
    blocks = refs[:host_count]
    down_ref, odd_ref, partial_ref, joint_ref, number_ref, over_ref = refs[host_count:-2]
    tiles, total = refs[-2:]
    heads = down_ref.shape[1] // HD
    rows_all = host_count * room
    size = room * HEAD_ROWS
    width = 256
    rank = LANES // 2
    lane = iota((8, LANES), 1)
    over = jnp.zeros((8, LANES), jnp.float32)
    for k in range(host_count):
        tiles[k * size : (k + 1) * size] = blocks[k][:size].astype(jnp.float32)
        tile = blocks[k][size:].astype(jnp.float32)
        over = jnp.maximum(over, jnp.where(lane == LANES - 1, tile, 0.0))
        for b in range(up_to(room, 8) // 8):
            rest = min(8, room - 8 * b)
            column = jnp.sum(jnp.where(lane == b, tile, 0.0), axis=1, keepdims=True)
            column = jnp.broadcast_to(column, (8, LANES))
            number_ref[k * room + 8 * b : k * room + 8 * b + rest] = column[:rest]
    over_ref[...] = over
    rows = jnp.concatenate(
        [tiles[pl.ds(j, rows_all, stride=HEAD_ROWS), :].astype(jnp.bfloat16) for j in range(heads)],
        axis=1,
    )
    number = number_ref[...]
    own = (iota(number.shape, 1) // rank).astype(jnp.float32) + 1.0
    for step in range(down_ref.shape[0] // width):
        product = lax.dot_general(
            rows,
            down_ref[step * width : (step + 1) * width],
            NT,
            preferred_element_type=jnp.float32,
        )
        add = jnp.zeros_like(number) if step == 0 else total[...]
        for i in range(width // LANES):
            piece = product[:, i * LANES : (i + 1) * LANES]
            first = 2.0 * (step * (width // LANES) + i)
            add = jnp.where(number == own + first, piece + add, add)
        total[...] = add
    full = total[...]
    full = full + pltpu.roll(full, rank, 1)
    half = rows_all // 2
    left = iota((half, LANES), 1) < rank
    partial_ref[...] = jnp.where(left, full[:half], full[half:]).astype(jnp.bfloat16)
    joint_ref[:half] = partial_ref[...]
    odd_rows = odd_ref.shape[0]
    for j in range(odd_ref.shape[1] // LANES):
        first = half + j * odd_rows
        joint_ref[first : first + odd_rows] = odd_ref[:, j * LANES : (j + 1) * LANES]


def shrink(blocks, down, odd, room):
    host_count = len(blocks)
    rows = host_count * room
    spec = pl.BlockSpec(memory_space=pltpu.VMEM)
    return pl.pallas_call(
        functools.partial(shrink_kernel, host_count, room),
        name="shrink",
        out_shape=(
            jax.ShapeDtypeStruct((rows // 2, LANES), jnp.bfloat16),
            jax.ShapeDtypeStruct((rows // 2 + odd.size // LANES, LANES), jnp.bfloat16),
            jax.ShapeDtypeStruct((rows, LANES), jnp.float32),
            jax.ShapeDtypeStruct((8, LANES), jnp.float32),
        ),
        in_specs=[spec] * (host_count + 2),
        out_specs=(spec,) * 4,
        scratch_shapes=[
            pltpu.VMEM((rows * HEAD_ROWS, HD), jnp.float32),
            pltpu.VMEM((rows, LANES), jnp.float32),
        ],
        compiler_params=pltpu.CompilerParams(vmem_limit_bytes=12 * MIB),
        cost_estimate=pl.CostEstimate(
            flops=2 * rows * down.size, bytes_accessed=2 * down.size, transcendentals=0
        ),
    )(*blocks, down, odd)


def expand_kernel(part_count, even_count, host_count, *refs):
    parts, refs = refs[:part_count], refs[part_count:]
    evens, (number_ref, up_ref), refs = refs[:even_count], refs[even_count:][:2], refs[even_count + 2 :]
    outs, sums, (spread, tiles) = refs[:host_count], refs[host_count:-2], refs[-2:]
    rows, columns = number_ref.shape[0], up_ref.shape[1]
    width = min(256, columns)
    rank = LANES // 2
    half = rows // 2
    full = parts[0][...].astype(jnp.float32)
    for p in parts[1:]:
        full = full + p[:half].astype(jnp.float32)
    other = pltpu.roll(full, rank, 1)
    left = iota(full.shape, 1) < rank
    both = jnp.concatenate(
        [jnp.where(left, full, other), jnp.where(left, other, full)], axis=0
    )
    number = number_ref[...]
    own = (iota(number.shape, 1) // rank).astype(jnp.float32) + 1.0
    for i in range(spread.shape[1] // LANES):
        spread[:, i * LANES : (i + 1) * LANES] = jnp.where(
            number == own + 2.0 * i, both, 0.0
        ).astype(jnp.bfloat16)
    if columns // HD < HEAD_ROWS:
        tiles[...] = jnp.zeros_like(tiles)
    for i in range(columns // width):
        result = jnp.dot(
            spread[...],
            up_ref[:, i * width : (i + 1) * width],
            preferred_element_type=jnp.float32,
        )
        for j in range(width // HD):
            tiles[pl.ds(i * (width // HD) + j, rows, stride=HEAD_ROWS), :] = result[
                :, j * HD : (j + 1) * HD
            ]
    size = rows // host_count * HEAD_ROWS
    for k in range(host_count):
        outs[k][...] = tiles[k * size : (k + 1) * size].astype(jnp.bfloat16)
    row_count = evens[0].shape[0]
    for i in range(even_count):
        for j in range(columns // LANES):
            first = half + (j * even_count + i) * row_count
            cut = slice(j * LANES, (j + 1) * LANES)
            sums[i][:, cut] = (
                evens[i][:, cut].astype(jnp.float32)
                + parts[1][first : first + row_count].astype(jnp.float32)
            ).astype(jnp.bfloat16)


def expand(parts, evens, number, up, host_count):
    rows = number.shape[0]
    depth, columns = up.shape
    spec = pl.BlockSpec(memory_space=pltpu.VMEM)
    block = jax.ShapeDtypeStruct((rows // host_count * HEAD_ROWS, HD), jnp.bfloat16)
    outs = pl.pallas_call(
        functools.partial(expand_kernel, len(parts), len(evens), host_count),
        name="expand",
        out_shape=[block] * host_count
        + [jax.ShapeDtypeStruct(e.shape, jnp.bfloat16) for e in evens],
        in_specs=[spec] * (len(parts) + len(evens) + 2),
        out_specs=[spec] * (host_count + len(evens)),
        scratch_shapes=[
            pltpu.VMEM((rows, depth), jnp.bfloat16),
            pltpu.VMEM((rows * HEAD_ROWS, HD), jnp.float32),
        ],
        compiler_params=pltpu.CompilerParams(vmem_limit_bytes=12 * MIB),
        cost_estimate=pl.CostEstimate(
            flops=2 * rows * up.size, bytes_accessed=2 * up.size, transcendentals=0
        ),
    )(*parts, *evens, number, up)
    return outs[:host_count], outs[host_count:]


def finish_kernel(base_count, back_count, place_ref, residual_ref, *refs):
    bases, backs = refs[:base_count], refs[base_count : base_count + back_count]
    more, (out_ref, tiles) = refs[base_count + back_count : -2], refs[-2:]
    columns = residual_ref.shape[1]
    size = backs[0].shape[0]
    for k in range(back_count):
        tiles[k * size : (k + 1) * size] = backs[k][...].astype(jnp.float32)
    used = back_count * size
    if used < tiles.shape[0]:
        tiles[used:] = jnp.zeros((tiles.shape[0] - used, HD), jnp.float32)
    place = place_ref[...]
    for j in range(columns // HD):
        cut = slice(j * HD, (j + 1) * HD)
        column = tiles[pl.ds(j, place.shape[1], stride=HEAD_ROWS), :].astype(jnp.bfloat16)
        total = jnp.dot(place, column, preferred_element_type=jnp.float32)
        for m in more:
            total = total + m[:, cut]
        total = residual_ref[:, cut].astype(jnp.float32) + ADAPTER_SCALE * total
        for b in bases:
            total = total + b[:, cut].astype(jnp.float32)
        out_ref[:, cut] = total.astype(jnp.bfloat16)


def finish(place, residual, bases, backs, *more):
    spec = pl.BlockSpec(memory_space=pltpu.VMEM)
    return pl.pallas_call(
        functools.partial(finish_kernel, len(bases), len(backs)),
        name="finish",
        out_shape=pltpu.HBM(residual.shape, jnp.bfloat16),
        in_specs=[spec] * (2 + len(bases) + len(backs) + len(more)),
        out_specs=spec,
        scratch_shapes=[
            pltpu.VMEM((place.shape[1] * HEAD_ROWS, HD), jnp.float32),
        ],
        compiler_params=pltpu.CompilerParams(vmem_limit_bytes=8 * MIB),
    )(place, residual, *bases, *backs, *more)


def swap(value, axis, k):
    size = lax.axis_size(axis)
    return lax.ppermute(value, axis, [(i, i ^ k) for i in range(size)])


def swap_all(values, axis, ks):
    return [v if k == 0 else swap(v, axis, k) for v, k in zip(values, ks)]


def second_pass(attended, down, up, stock, slots, room, rest):
    owned_total, rank, feature_here = down.shape
    host_count = lax.axis_size("hst")
    tp_count = lax.axis_size("tp")
    row_count = attended.shape[0]
    adapter = stock[slots]
    owner = adapter // owned_total
    order = jnp.arange(row_count)
    same = (owner[:, None] == owner[None, :]) & (order[None, :] < order[:, None])
    before = jnp.sum(same, axis=1)
    target = jnp.where(before >= room, owner * rest + before - room, -1)
    place = (target[:, None] == jnp.arange(host_count * rest)[None, :]).astype(jnp.float32)
    number = (adapter % owned_total + 1).astype(jnp.float32)
    numbers = jnp.broadcast_to((place.T @ number)[:, None], (host_count * rest, LANES))
    rows = jnp.dot(
        place.T.astype(jnp.bfloat16), attended, preferred_element_type=jnp.float32
    ).astype(jnp.bfloat16)
    rows = jnp.concatenate([rows, numbers.astype(jnp.bfloat16)], axis=1)
    rows = lax.all_to_all(rows, "hst", split_axis=0, concat_axis=0, tiled=True)
    number = rows[:, feature_here].astype(jnp.int32)
    rows = rows[:, :feature_here]
    uses = number[:, None] == jnp.arange(1, owned_total + 1)[None, :]
    product = jnp.einsum("rd,akd->rak", rows, down, preferred_element_type=jnp.float32)
    partial_sum = jnp.sum(jnp.where(uses[:, :, None], product, 0), axis=1)
    shrunk = sum([partial_sum] + [swap(partial_sum, "tp", k) for k in range(1, tp_count)])
    spread = jnp.where(uses[:, :, None], shrunk.astype(jnp.bfloat16)[:, None, :], 0)
    raised = jnp.einsum("rak,aki->ri", spread, up, preferred_element_type=jnp.float32)
    back = lax.all_to_all(
        raised.astype(jnp.bfloat16), "hst", split_axis=0, concat_axis=0, tiled=True
    )
    return jnp.dot(place.astype(jnp.bfloat16), back, preferred_element_type=jnp.float32)


def local(
    queries,
    key_page_cache,
    value_page_cache,
    request_pages,
    context_length,
    output_weight,
    adapter_down_weight,
    adapter_up_weight,
    residual,
    host_slot_adapter,
    request_slot,
):
    owned_total, rank, feature_here = adapter_down_weight.shape
    host_count = lax.axis_size("hst")
    tp_count = lax.axis_size("tp")
    slot_total = host_slot_adapter.shape[0]
    most = pair_rows(slot_total, host_count)
    room = min(FIRST, most)
    (attended, place, down, up), blocks = attend(
        queries,
        key_page_cache,
        value_page_cache,
        request_pages.T,
        context_length,
        request_slot.reshape(1, -1),
        host_slot_adapter.reshape(1, slot_total),
        adapter_down_weight.reshape(owned_total * rank, feature_here),
        adapter_up_weight.reshape(owned_total * rank, -1),
        owned_total,
        host_count,
        room,
    )
    row_count = attended.shape[0]
    ks = partners(host_count)
    blocks = swap_all(blocks, "hst", ks)
    evens = tp_count // 2
    one = jax.ShapeDtypeStruct((row_count, feature_here), jnp.bfloat16)
    odd = jax.ShapeDtypeStruct((evens * row_count, feature_here), jnp.bfloat16)
    odd = base_half(odd_kernel, "base_odd", attended, output_weight, odd)
    blocks, odd = lax.optimization_barrier((blocks, odd))
    partial_sum, joint, number, over = shrink(blocks, down, odd, room)
    parts = [partial_sum, joint] + [partial_sum] * (tp_count - 2)
    parts = swap_all(parts, "tp", range(tp_count))
    even = base_half(even_kernel, "base_even", attended, output_weight, [one] * evens)
    parts, even = lax.optimization_barrier((parts, even))
    raised, bases = expand(parts, even, number, up, host_count)
    bases = swap_all(bases, "tp", range(0, tp_count, 2))
    late = host_count // 2 + 1
    last, bases = lax.optimization_barrier((raised[late:], bases))
    backs = swap_all([*raised[:late], *last], "hst", ks)
    if room == most:
        return finish(place, residual, bases, backs)

    def with_second(bases, backs):
        more = second_pass(
            attended,
            adapter_down_weight,
            adapter_up_weight,
            host_slot_adapter,
            request_slot[:, 0],
            room,
            up_to(most - room, 16),
        )
        return finish(place, residual, bases, backs, more)

    def first_only(bases, backs):
        return finish(place, residual, bases, backs)

    return lax.cond(jnp.max(over) > 0, with_second, first_only, bases, backs)


def solution(mesh):
    in_specs = (
        P("hst", "tp"),
        P("hst", None, "tp"),
        P("hst", None, "tp"),
        P("hst", None),
        P("hst"),
        P("tp", None),
        P("hst", None, "tp"),
        P("hst", None, "tp"),
        P("hst", "tp"),
        P("hst"),
        P("hst", None),
    )
    out_specs = P("hst", "tp")
    return jax.shard_map(local, mesh=mesh, in_specs=in_specs, out_specs=out_specs, check_vma=False)
```
